32 devices in a mesh: wide: 8 (over z, y), narrow: 4 (over x, core).
Axes of the slice: x: 2, y: 2, z: 4, core: 2. Of those that a mesh axis runs over, the one named last changes fastest.
Arguments:
- layer_input_rows: bfloat16 [16384, 4096], P('wide', 'narrow'), may hold values from -6 to 6
- output_gradient_rows: bfloat16 [16384, 4096], P('wide', 'narrow'), may hold values from -60 to 60
- adapter_up_weight: bfloat16 [4096, 128], P('narrow'), may hold values from -0.09375 to 0.09375
- input_side_projection: bfloat16 [4096, 128], P('narrow'), may hold values from -0.09375 to 0.09375
- rank_side_projection: bfloat16 [128, 64], replicated, may hold values from -6 to 6
- lengths: int32 [512], P('wide'), may hold values from 1 to 32, 10240 in all
- program_output_index: int32 [512], replicated, may hold values from 0 to 511, each once
- targets: bfloat16 [16384, 8192], P('wide', 'narrow'), may hold values from -650 to 650
Outputs:
- scores: float32 [512, 16384], P('narrow', 'wide')
The draws below stay inside these ranges and needn't reach their ends.
Inputs may be any that keep to these rules, and one draw needn't show every extreme that they name: Program s uses its first lengths[s] token rows; some program uses all 32. `program_output_index`: each output row is named by exactly one program.
All inputs are finite; a program needn't handle non-finite values. No bound on the sum of `lengths` on one device may be relied on, other than what follows from the above.
Results may differ from the reference program's by a relative error of at most 0.025.
Values may be sent and summed in bfloat16 or wider, within the bound.
No kernel may reach another device: no remote copies, remote signals or barrier semaphores. Data moves between devices by JAX's collectives and lax.ppermute only.
A program may use at most 128 MiB of HBM per device.

```python
import math
import jax
import jax.numpy as jnp
import numpy as np
from jax import lax

D = 4096
OUTPUT_WIDTH = 4096
ADAPTER_RANK = 128
K1 = 128
K2 = 64
K = 8192
KPART = 2048
L = 32
TGTB = 2048
S = 512
TGT = 16384
TOKENS = 16384
N_WIDE = 8
N_NARROW = 4


def column_scales(key, number):
    ramp = jnp.arange(number, dtype=jnp.float32) / max(number - 1, 1)
    rough = jax.random.uniform(key, (number,), jnp.float32)
    return jnp.exp(jnp.log(3.0) * ramp + jnp.log(3.3) * rough)


def draw_rank_side_projection(key, part):
    scales = column_scales(jax.random.fold_in(key, 11), K2)
    base = jax.random.truncated_normal(jax.random.fold_in(key, 12), -6.0, 6.0, (ADAPTER_RANK, K2), jnp.float32)
    return (base * scales[None, :] / math.sqrt(ADAPTER_RANK)).astype(jnp.bfloat16)


def draw_output_gradient_rows(key, part):
    row_scales = jnp.exp(jnp.log(10.0) * jax.random.uniform(jax.random.fold_in(key, 21), (TOKENS, 1), jnp.float32))
    base = jax.random.truncated_normal(jax.random.fold_in(key, 23), -6.0, 6.0, (TOKENS, OUTPUT_WIDTH), jnp.float32)
    return (base * row_scales).astype(jnp.bfloat16)


def draw_targets(key, part):
    scales = jnp.repeat(column_scales(jax.random.fold_in(key, 31), K2), K1)
    row_scales = jnp.exp(jnp.log(10.0) * jax.random.uniform(jax.random.fold_in(key, 32), (TGT, 1), jnp.float32))
    base = jax.random.truncated_normal(jax.random.fold_in(key, 34), -6.0, 6.0, (TGT, K), jnp.float32)
    return (base * scales[None, :] * row_scales).astype(jnp.bfloat16)


def level_of(rng, extent, shards, least, top_value):
    factor_of = 1.0
    for dim, blocks in shards:
        heights = jax.random.uniform(jax.random.fold_in(jax.random.fold_in(rng, 6), dim), (blocks,), jnp.float32, least / len(shards), top_value / len(shards))
        factor_of = factor_of * jnp.repeat(jnp.exp(heights), extent[dim] // blocks).reshape((-1,) + (1,) * (len(extent) - 1 - dim))
    return factor_of


def profile(count, total, most, slope):
    portions = [(1 << 20) // math.isqrt(standing ** slope) + 1 for standing in range(2, count + 1)]
    spare, counts = total - most - (count - 1), [1] * (count - 1)
    while spare > 0:
        candidates = [i for i in range(count - 1) if counts[i] < most]
        mass, remaining = sum([portions[i] for i in candidates]), spare
        for i in candidates:
            addition = min(most - counts[i], max(1, remaining * portions[i] // mass), spare)
            counts[i] = counts[i] + addition
            spare = spare - addition
    return np.array([most] + counts)


def ragged(rng, count, total, most, skew):
    if count == 2:
        one = jax.random.randint(rng, (), max(1, total - most), min(most, total - 1) + 1)
        return jnp.stack([one, total - one])
    sizes = jnp.asarray(profile(count, total, most, skew), jnp.int32)
    pairs = (count - 1) // 2
    giver, taker = sizes[1:1 + 2 * pairs:2], sizes[2:2 + 2 * pairs:2]
    margin = jnp.minimum(giver - 1, most - taker)
    moved = jax.random.randint(jax.random.fold_in(rng, 1), (pairs,), 0, 1 << 20) % (margin + 1)
    sizes = sizes.at[1:1 + 2 * pairs:2].set(giver - moved).at[2:2 + 2 * pairs:2].set(taker + moved)
    return sizes[jax.random.permutation(jax.random.fold_in(rng, 2), count)]


def scatter_about(key, dims, scale, limit, split=(), kind=jnp.bfloat16):
    array = scale * jax.random.normal(key, dims, jnp.float32)
    if split:
        array = array * level_of(key, dims, split, -0.22, 0.18)
    return jnp.clip(array, -limit, limit).astype(kind)


def setup_inputs(seed: int = 0) -> dict:
    keys = jax.random.split(jax.random.key(seed), 9)
    layer_input_rows = scatter_about(keys[0], (TOKENS, D), 1.0, 6.0, ((0, 8), (1, 4)))
    output_gradient_rows = draw_output_gradient_rows(jax.random.fold_in(keys[8], 71), 0)
    adapter_up_weight = scatter_about(keys[2], (OUTPUT_WIDTH, ADAPTER_RANK), OUTPUT_WIDTH ** -0.5, 0.09375, ((0, 4),))
    input_side_projection = scatter_about(keys[3], (D, K1), D ** -0.5, 0.09375, ((0, 4),))
    rank_side_projection = draw_rank_side_projection(jax.random.fold_in(keys[8], 71), 0)
    lengths = ragged(keys[5], S, S * L * 5 // 8, L, 1).astype(jnp.int32)
    program_output_index = jax.random.permutation(keys[6], S).astype(jnp.int32)
    targets = draw_targets(jax.random.fold_in(keys[8], 71), 0)
    return {"layer_input_rows": layer_input_rows, "output_gradient_rows": output_gradient_rows, "adapter_up_weight": adapter_up_weight, "input_side_projection": input_side_projection, "rank_side_projection": rank_side_projection, "lengths": lengths, "program_output_index": program_output_index, "targets": targets}


epsilon = 1e-06

def reference(layer_input_rows, output_gradient_rows, adapter_up_weight, input_side_projection, rank_side_projection, lengths, program_output_index, targets):
    reduced_sums = jnp.dot(output_gradient_rows, adapter_up_weight, preferred_element_type=jnp.float32)
    out_side = jnp.dot(reduced_sums, rank_side_projection.astype(jnp.float32), precision=lax.Precision.HIGHEST)
    in_side = jnp.dot(layer_input_rows, input_side_projection, preferred_element_type=jnp.float32)
    positions = jnp.arange(L, dtype=jnp.int32)
    live_rows = (positions[None, :] < lengths[:, None]).astype(jnp.float32)
    weighted = out_side.reshape(S, L, K2) * live_rows[:, :, None]
    features = jnp.einsum('sla,slb->sab', weighted, in_side.reshape(S, L, K1), precision=lax.Precision.HIGHEST).reshape(S, K)
    squares = lax.optimization_barrier(jnp.sum(features * features, axis=1))
    unit_rows = (features * lax.rsqrt(squares + epsilon)[:, None]).astype(jnp.bfloat16)
    row_order = jnp.argsort(program_output_index).astype(jnp.int32)
    ordered = jnp.take(unit_rows, row_order, axis=0)
    blocks = targets.reshape(N_WIDE, TGTB, K)

    def score_block(target_block):
        wide_block = target_block.astype(jnp.float32)
        target_squares = lax.optimization_barrier(jnp.sum(wide_block * wide_block, axis=1))
        target_unit = (wide_block * lax.rsqrt(target_squares + epsilon)[:, None]).astype(jnp.bfloat16)
        summed = jnp.zeros((S, TGTB), jnp.float32)
        for quarter_index in range(N_NARROW):
            lower = quarter_index * KPART
            quarter_part = jnp.dot(ordered[:, lower:lower + KPART], target_unit[:, lower:lower + KPART].T, preferred_element_type=jnp.float32).astype(jnp.bfloat16)
            summed = summed + quarter_part.astype(jnp.float32)
        return summed * math.sqrt(K)
    stacked = lax.map(score_block, blocks)
    return jnp.transpose(stacked, (1, 0, 2)).reshape(S, TGT)
```

```python
import math

import jax
import jax.numpy as jnp
from jax import lax
from jax.sharding import PartitionSpec as P

epsilon = 1e-06


def exchange(array, axis, bit):
    count = lax.axis_size(axis)
    return lax.ppermute(array, axis, [(i, i ^ bit) for i in range(count)])


def pick(array, index):
    return lax.dynamic_index_in_dim(array, index, 0, keepdims=False)


def gather_blocks(block):
    count = lax.axis_size("wide")
    held = {0: block}
    bit = count // 2
    while bit:
        for k in list(held):
            held[k | bit] = exchange(held[k], "wide", bit)
        bit //= 2
    return [held[k] for k in range(count)]


def shards(
    layer_input_rows,
    output_gradient_rows,
    adapter_up_weight,
    input_side_projection,
    rank_side_projection,
    lengths,
    program_output_index,
    targets,
):
    f32, bf16 = jnp.float32, jnp.bfloat16
    wide_count, narrow_count = lax.axis_size("wide"), lax.axis_size("narrow")
    w, n = lax.axis_index("wide"), lax.axis_index("narrow")
    core, x = n % 2, n // 2
    programs = lengths.shape[0]
    length = layer_input_rows.shape[0] // programs
    in_width = input_side_projection.shape[1]
    out_width = rank_side_projection.shape[1]
    quarter = out_width // narrow_count
    half = programs // 2

    reduced = jnp.dot(output_gradient_rows, adapter_up_weight, preferred_element_type=f32)
    out_part = jnp.dot(reduced, rank_side_projection.astype(f32), precision=lax.Precision.HIGHEST)
    in_part = jnp.dot(layer_input_rows, input_side_projection, preferred_element_type=f32)
    both = jnp.concatenate([in_part, out_part], axis=1).astype(bf16)
    both = both.reshape(2, half * length, in_width + out_width)

    chip = pick(both, core).astype(f32) + exchange(pick(both, 1 - core), "narrow", 1).astype(f32)
    chip_in = chip[:, :in_width]
    chip_out = chip[:, in_width:].reshape(-1, 2, 2 * quarter).transpose(1, 0, 2)
    sent = jnp.concatenate([chip_in, pick(chip_out, 1 - x)], axis=1).astype(bf16)
    came = exchange(sent, "narrow", 2).astype(f32)
    in_sum = chip_in + came[:, :in_width]
    out_sum = pick(chip_out, x) + came[:, in_width:]

    half_lengths = pick(lengths.reshape(2, half), core)
    live = lax.broadcasted_iota(jnp.int32, (half, length), 1) < half_lengths[:, None]
    weighted = out_sum.reshape(half, length, -1) * live[:, :, None].astype(f32)
    features = jnp.einsum(
        "sla,slb->sab", weighted, in_sum.reshape(half, length, -1), precision=lax.Precision.HIGHEST
    )
    features = features.reshape(half, 2, -1).transpose(1, 0, 2).astype(bf16)
    other = exchange(pick(features, 1 - core), "narrow", 1)
    mine = pick(features, core)
    block = jnp.concatenate([jnp.where(core == 0, mine, other), jnp.where(core == 0, other, mine)], 0)

    wide_targets = targets.astype(f32)
    target_squares = jnp.sum(wide_targets * wide_targets, axis=1)
    target_squares = target_squares + exchange(target_squares, "narrow", 1)
    target_squares = target_squares + exchange(target_squares, "narrow", 2)

    gathered = jnp.concatenate(gather_blocks(block), axis=0)
    order = program_output_index.reshape(wide_count, programs)
    order = jnp.take(order, w ^ jnp.arange(wide_count), axis=0).reshape(-1)
    rows = order.shape[0] // narrow_count
    contract = (((1,), (1,)), ((), ()))

    def partial(x_index, core_index):
        first = (x_index * 2 + core_index) * rows
        chosen = (lax.broadcasted_iota(jnp.int32, (rows, order.shape[0]), 0) + first == order[None, :])
        ordered = jnp.dot(chosen.astype(bf16), gathered, preferred_element_type=f32)
        squares = jnp.sum(ordered * ordered, axis=1)
        return lax.dot_general(
            ordered.astype(bf16), targets, contract, preferred_element_type=f32
        ), squares

    far_send, far_send_sq = partial(1 - x, 1 - core)
    far_keep, far_keep_sq = partial(1 - x, core)
    far = far_keep + exchange(far_send.astype(bf16), "narrow", 1).astype(f32)
    far_sq = far_keep_sq + exchange(far_send_sq, "narrow", 1)
    near_send, near_send_sq = partial(x, 1 - core)
    near_keep, near_keep_sq = partial(x, core)
    near = near_keep + exchange(near_send.astype(bf16), "narrow", 1).astype(f32)
    near_sq = near_keep_sq + exchange(near_send_sq, "narrow", 1)
    total = near + exchange(far.astype(bf16), "narrow", 2).astype(f32)
    squares = near_sq + exchange(far_sq, "narrow", 2)
    root_count = math.sqrt(float(targets.shape[1] * narrow_count))
    row_scale = lax.rsqrt(squares + epsilon) * root_count
    return total * row_scale[:, None] * lax.rsqrt(target_squares + epsilon)[None, :]


def solution(mesh):
    return jax.shard_map(
        shards,
        mesh=mesh,
        in_specs=(
            P("wide", "narrow"),
            P("wide", "narrow"),
            P("narrow", None),
            P("narrow", None),
            P(),
            P("wide"),
            P(),
            P("wide", "narrow"),
        ),
        out_specs=P("narrow", "wide"),
        check_vma=False,
    )
```

```python
import functools
import math

import jax
import jax.numpy as jnp
from jax import lax
from jax.experimental import pallas as pl
from jax.experimental.pallas import tpu as pltpu
from jax.sharding import PartitionSpec as P

epsilon = 1e-06
chunks = 2
lanes = 128
f32, bf16 = jnp.float32, jnp.bfloat16
nt = (((1,), (1,)), ((), ()))


def params():
    return pltpu.CompilerParams(vmem_limit_bytes=40 * 1024 * 1024)


def cost(flops, moved):
    return pl.CostEstimate(flops=flops, bytes_accessed=moved, transcendentals=0)


def exchange(array, axis, bit):
    count = lax.axis_size(axis)
    return lax.ppermute(array, axis, [(i, i ^ bit) for i in range(count)])


def gather_blocks(block):
    count = lax.axis_size("wide")
    held = {0: block}
    bit = count // 2
    while bit:
        for k in list(held):
            held[k | bit] = exchange(held[k], "wide", bit)
        bit //= 2
    return [held[k] for k in range(count)]


def project_kernel(place, x_ref, g_ref, w_ref, up_ref, rank_ref, send_ref, keep_ref):
    half, step = pl.program_id(0), pl.program_id(1)
    sub = x_ref.shape[0]
    tokens = pl.num_programs(1) * sub
    out_width = rank_ref.shape[0] // 2
    stack = tokens // lanes * out_width
    in_part = jnp.dot(x_ref[...], w_ref[...], preferred_element_type=f32)
    reduced = jnp.dot(g_ref[...], up_ref[...], preferred_element_type=f32)
    out_part = lax.dot_general(
        rank_ref[...], reduced, nt, preferred_element_type=f32, precision=lax.Precision.HIGHEST
    )

    def store(ref):
        ref[pl.ds(step * sub, sub), :] = in_part.astype(ref.dtype)
        for x in range(2):
            for piece in range(sub // lanes):
                row = tokens + x * stack + (step * (sub // lanes) + piece) * out_width
                ref[pl.ds(pl.multiple_of(row, out_width), out_width), :] = out_part[
                    x * out_width : (x + 1) * out_width, piece * lanes : (piece + 1) * lanes
                ].astype(ref.dtype)

    @pl.when(half == 0)
    def _():
        store(send_ref)

    @pl.when(half == 1)
    def _():
        store(keep_ref)


def project(chunk, place, x, g, w, up, rank):
    tokens = x.shape[0] // chunks // 2
    sub = min(256, tokens)
    steps = tokens // sub
    depth = x.shape[1]
    rows = tokens + 2 * (tokens // lanes) * (rank.shape[0] // 2)

    def block(half, step, place):
        mine = place[0] + (1 - half) * (1 - 2 * place[0])
        return ((chunk * 2 + mine) * steps + step, 0)

    def whole(half, step, place):
        return (0, 0)

    return pl.pallas_call(
        project_kernel,
        grid_spec=pltpu.PrefetchScalarGridSpec(
            num_scalar_prefetch=1,
            grid=(2, steps),
            in_specs=[
                pl.BlockSpec((sub, depth), block),
                pl.BlockSpec((sub, depth), block),
                pl.BlockSpec(w.shape, whole),
                pl.BlockSpec(up.shape, whole),
                pl.BlockSpec(rank.shape, whole),
            ],
            out_specs=[pl.BlockSpec((rows, lanes), whole), pl.BlockSpec((rows, lanes), whole)],
        ),
        out_shape=[
            jax.ShapeDtypeStruct((rows, lanes), bf16),
            jax.ShapeDtypeStruct((rows, lanes), f32),
        ],
        compiler_params=params(),
        cost_estimate=cost(8 * tokens * depth * lanes, 8 * tokens * depth),
        name="project",
    )(place, x, g, w, up, rank)


def core_sum_kernel(place, keep_ref, came_ref, send_ref, left_ref):
    rows = keep_ref.shape[0]
    final = send_ref.shape[0]
    stack = rows - final
    tokens = final - stack
    x = place[1]
    total = keep_ref[:tokens, :] + came_ref[:tokens, :].astype(f32)
    send_ref[:tokens, :] = total.astype(bf16)
    left_ref[:tokens, :] = total
    far = pl.ds(pl.multiple_of(tokens + (1 - x) * stack, stack), stack)
    near = pl.ds(pl.multiple_of(tokens + x * stack, stack), stack)
    send_ref[tokens:, :] = (keep_ref[far, :] + came_ref[far, :].astype(f32)).astype(bf16)
    left_ref[tokens:, :] = keep_ref[near, :] + came_ref[near, :].astype(f32)


def core_sum(place, keep, came, tokens):
    rows = keep.shape[0]
    final = tokens + (rows - tokens) // 2
    vmem = pl.BlockSpec(memory_space=pltpu.VMEM)
    return pl.pallas_call(
        core_sum_kernel,
        in_specs=[pl.BlockSpec(memory_space=pltpu.SMEM), vmem, vmem],
        out_specs=[vmem, vmem],
        out_shape=[
            jax.ShapeDtypeStruct((final, lanes), bf16),
            jax.ShapeDtypeStruct((final, lanes), f32),
        ],
        compiler_params=params(),
        cost_estimate=cost(rows * lanes, 12 * rows * lanes),
        name="core_sum",
    )(place, keep, came)


def feature_kernel(first, programs, place, lengths, left_ref, came_ref, mine_ref, other_ref, held):
    core = place[0]
    quarter = mine_ref.shape[0]
    out_width = 2 * quarter
    final = left_ref.shape[0]
    tokens = final * lanes // (lanes + out_width)
    length = tokens // programs
    in_sum = (left_ref[:tokens, :] + came_ref[:tokens, :].astype(f32)).astype(bf16)
    out_sum = left_ref[tokens:, :] + came_ref[tokens:, :].astype(f32)
    out_rows = jnp.concatenate(
        [out_sum[i * out_width : (i + 1) * out_width, :] for i in range(tokens // lanes)], axis=1
    )
    program = lax.broadcasted_iota(jnp.int32, (programs, tokens), 0)
    token = lax.broadcasted_iota(jnp.int32, (programs, tokens), 1) - program * length
    limit = jnp.zeros((programs, tokens), jnp.int32)
    for s in range(programs):
        limit = jnp.where(program == s, lengths[first + core * programs + s], limit)
    live = ((token >= 0) & (token < limit)).astype(f32)
    spread = (out_rows[:, None, :] * live[None, :, :]).reshape(out_width * programs, tokens)
    made = jnp.dot(spread.astype(bf16), in_sum, preferred_element_type=f32)
    held[...] = made.reshape(out_width, programs, lanes)
    mine_ref[...] = held[pl.ds(core * quarter, quarter), :, :].astype(bf16)
    other_ref[...] = held[pl.ds((1 - core) * quarter, quarter), :, :].astype(bf16)


def make_features(first, programs, quarter, place, lengths, left, came):
    vmem = pl.BlockSpec(memory_space=pltpu.VMEM)
    smem = pl.BlockSpec(memory_space=pltpu.SMEM)
    shape = jax.ShapeDtypeStruct((quarter, programs, lanes), bf16)
    return pl.pallas_call(
        functools.partial(feature_kernel, first, programs),
        in_specs=[smem, smem, vmem, vmem],
        out_specs=[vmem, vmem],
        out_shape=[shape, shape],
        scratch_shapes=[pltpu.VMEM((2 * quarter, programs, lanes), f32)],
        compiler_params=params(),
        cost_estimate=cost(10**8, 8 * left.size),
        name="features",
    )(place, lengths, left, came)


def score_kernel(count, squares_too, place, order_ref, *refs):
    pieces, refs = refs[:count], refs[count:]
    targets_ref, send_ref, keep_ref, squares_ref = refs[:4]
    ordered = refs[-1]
    rows = send_ref.shape[0]
    core, x = place[0], place[2]

    @pl.when(pl.program_id(0) == 0)
    def _():
        position_rows = order_ref[...]
        quarter = pieces[0].shape[1]
        row = lax.broadcasted_iota(jnp.int32, (2 * rows, position_rows.shape[1]), 0)
        first = jnp.where(row < rows, (x * 2 + 1 - core) * rows, (x * 2 + core) * rows - rows)
        chosen = (row + first == position_rows).astype(bf16)
        totals = jnp.zeros((2 * rows, lanes), f32)
        for a in range(0, quarter, 2):
            block = jnp.concatenate(
                [
                    jnp.concatenate([piece[i, a + d] for piece in pieces for i in range(2)], axis=0)
                    for d in range(2)
                ],
                axis=1,
            )
            found = jnp.dot(chosen, block, preferred_element_type=f32)
            ordered[:, a * lanes : (a + 2) * lanes] = found.astype(bf16)
            totals += found[:, :lanes] * found[:, :lanes] + found[:, lanes:] * found[:, lanes:]
        squares_ref[...] = jnp.sum(totals.T, axis=0, keepdims=True)

    block = targets_ref[...]
    scores = lax.dot_general(ordered[...], block, nt, preferred_element_type=f32).astype(bf16)
    send_ref[...] = scores[:rows, :]
    keep_ref[...] = scores[rows:, :]
    if squares_too:
        wide = block.astype(f32)
        wide = wide * wide
        totals = wide[:, :lanes]
        for k in range(1, wide.shape[1] // lanes):
            totals += wide[:, k * lanes : (k + 1) * lanes]
        refs[4][...] = jnp.sum(totals.T, axis=0, keepdims=True)


def partial_scores(squares_too, place, order, pieces, targets, rows):
    columns, depth = targets.shape
    tile = min(512, columns)
    whole = lambda *shape: pl.BlockSpec(shape, lambda j, place: (0,) * len(shape))
    strip = lambda height: pl.BlockSpec((height, tile), lambda j, place: (0, j))
    out_specs = [strip(rows), strip(rows), whole(1, 2 * rows)]
    out_shape = [
        jax.ShapeDtypeStruct((rows, columns), bf16),
        jax.ShapeDtypeStruct((rows, columns), bf16),
        jax.ShapeDtypeStruct((1, 2 * rows), f32),
    ]
    if squares_too:
        out_specs.append(strip(1))
        out_shape.append(jax.ShapeDtypeStruct((1, columns), f32))
    return pl.pallas_call(
        functools.partial(score_kernel, len(pieces), squares_too),
        grid_spec=pltpu.PrefetchScalarGridSpec(
            num_scalar_prefetch=1,
            grid=(columns // tile,),
            in_specs=[whole(*order.shape)]
            + [whole(*piece.shape) for piece in pieces]
            + [pl.BlockSpec((tile, depth), lambda j, place: (j, 0))],
            out_specs=out_specs,
            scratch_shapes=[pltpu.VMEM((2 * rows, depth), bf16)],
        ),
        out_shape=out_shape,
        compiler_params=params(),
        cost_estimate=cost(4 * rows * columns * depth, 2 * columns * depth),
        name="scores",
    )(place, order, *pieces, targets)


def shards(
    layer_input_rows,
    output_gradient_rows,
    adapter_up_weight,
    input_side_projection,
    rank_side_projection,
    lengths,
    program_output_index,
    targets,
):
    wide_count, narrow_count = lax.axis_size("wide"), lax.axis_size("narrow")
    w, n = lax.axis_index("wide"), lax.axis_index("narrow")
    core, x = n % 2, n // 2
    programs = lengths.shape[0]
    length = layer_input_rows.shape[0] // programs
    quarter = rank_side_projection.shape[1] // narrow_count
    share = programs // chunks // 2
    tokens = share * length
    place = jnp.stack([core, x]).astype(jnp.int32)
    rank = rank_side_projection.astype(f32).T

    pieces = []
    for chunk in range(chunks):
        send, keep = project(
            chunk,
            place,
            layer_input_rows,
            output_gradient_rows,
            input_side_projection,
            adapter_up_weight,
            rank,
        )
        send, left = core_sum(place, keep, exchange(send, "narrow", 1), tokens)
        came = exchange(send, "narrow", 2)
        mine, other = make_features(
            chunk * 2 * share, share, quarter, place, lengths, left, came
        )
        block = jnp.stack([mine, exchange(other, "narrow", 1)])
        pieces.append(gather_blocks(block))

    order = program_output_index.reshape(wide_count, chunks, 2, share)
    order = jnp.take(order, w ^ jnp.arange(wide_count), axis=0)
    order = jnp.take(order, core ^ jnp.arange(2), axis=2)
    order = order.transpose(1, 0, 2, 3).reshape(1, -1)
    pieces = [piece for chunk in pieces for piece in chunk]
    rows = order.shape[1] // narrow_count

    def scores(squares_too, x_index):
        where = jnp.stack([core, x, x_index]).astype(jnp.int32)
        return partial_scores(squares_too, where, order, pieces, targets, rows)

    far_send, far_keep, far_squares = scores(False, 1 - x)
    far = (far_keep.astype(f32) + exchange(far_send, "narrow", 1).astype(f32)).astype(bf16)
    far = exchange(far, "narrow", 2)
    near_send, near_keep, near_squares, target_squares = scores(True, x)
    near = near_keep.astype(f32) + exchange(near_send, "narrow", 1).astype(f32)

    far_squares = far_squares.reshape(2, rows)
    near_squares = near_squares.reshape(2, rows)
    groups = jnp.stack([far_squares, near_squares])
    groups = jnp.where(x == 1, groups, groups[::-1])
    groups = jnp.where(core == 1, groups, groups[:, ::-1])
    squares = jnp.concatenate([groups.reshape(-1), target_squares.reshape(-1)])
    squares = squares + exchange(squares, "narrow", 1)
    squares = squares + exchange(squares, "narrow", 2)
    row_squares = lax.dynamic_slice_in_dim(squares, n * rows, rows, 0)
    target_squares = squares[narrow_count * rows :]
    root_count = math.sqrt(float(targets.shape[1] * narrow_count))
    row_scale = lax.rsqrt(row_squares + epsilon) * root_count
    column_scale = lax.rsqrt(target_squares + epsilon)
    return (near + far.astype(f32)) * row_scale[:, None] * column_scale[None, :]


def solution(mesh):
    return jax.shard_map(
        shards,
        mesh=mesh,
        in_specs=(
            P("wide", "narrow"),
            P("wide", "narrow"),
            P("narrow", None),
            P("narrow", None),
            P(),
            P("wide"),
            P(),
            P("wide", "narrow"),
        ),
        out_specs=P("narrow", "wide"),
        check_vma=False,
    )
```

```python
import functools
import math

import jax
import jax.numpy as jnp
from jax import lax
from jax.experimental import pallas as pl
from jax.experimental.pallas import tpu as pltpu
from jax.sharding import PartitionSpec as P

epsilon = 1e-06
lanes = 128
f32, bf16 = jnp.float32, jnp.bfloat16
nt = (((1,), (1,)), ((), ()))


def params(mebibytes):
    return pltpu.CompilerParams(vmem_limit_bytes=int(mebibytes * 1024 * 1024))


def cost(flops, moved):
    return pl.CostEstimate(flops=flops, bytes_accessed=moved, transcendentals=0)


def exchange(array, axis, bit):
    count = lax.axis_size(axis)
    return lax.ppermute(array, axis, [(i, i ^ bit) for i in range(count)])


def after(array, *others):
    return lax.optimization_barrier((array,) + others)[0]


def gather_blocks(block):
    count = lax.axis_size("wide")
    held = {0: block, 1: exchange(block, "wide", 1)}
    bit = count // 2
    if count == 8:
        held[2], held[4] = exchange(block, "wide", 2), exchange(block, "wide", 4)
        held[6] = exchange(held[4], "wide", 2)
        held[5] = exchange(after(held[4], held[1], held[2]), "wide", 1)
        held[7] = exchange(held[6], "wide", 1)
        held[3] = exchange(after(held[1], held[6]), "wide", 2)
        return [held[k] for k in range(count)]
    while bit > 1:
        for k in [k for k in held if k % 2 == 0]:
            held[k | bit] = exchange(held[k], "wide", bit)
        bit //= 2
    for k in range(2, count, 2):
        held[k | 1] = exchange(held[k], "wide", 1)
    return [held[k] for k in range(count)]


def position():
    n = lax.axis_index("narrow")
    return n % 2, n // 2


def project_kernel(mine, x_hbm, g_hbm, w_hbm, up_hbm, rank_hbm, out_ref, x, g, w, up, rank, sems):
    core, _ = position()
    half = core if mine else 1 - core
    steps, sub = x.shape[:2]
    tokens = steps * sub
    out_width = rank.shape[0] // 2
    stack = tokens // lanes * out_width

    def copies(i):
        rows = pl.ds(pl.multiple_of((half * steps + i) * sub, sub), sub)
        return [
            pltpu.make_async_copy(x_hbm.at[rows, :], x.at[i], sems.at[2 * i]),
            pltpu.make_async_copy(g_hbm.at[rows, :], g.at[i], sems.at[2 * i + 1]),
        ]

    weights = [
        pltpu.make_async_copy(w_hbm, w, sems.at[2 * steps]),
        pltpu.make_async_copy(up_hbm, up, sems.at[2 * steps + 1]),
        pltpu.make_async_copy(rank_hbm, rank, sems.at[2 * steps + 2]),
    ]
    started = [copies(i) for i in range(steps)]
    for copy in weights + [copy for pair in started for copy in pair]:
        copy.start()
    for copy in weights:
        copy.wait()
    rank_twice = jnp.concatenate([rank[...], rank[...]], axis=1)
    for i in range(steps):
        for copy in started[i]:
            copy.wait()
        in_part = jnp.dot(x[i], w[...], preferred_element_type=f32)
        reduced = jnp.dot(g[i], up[...], preferred_element_type=f32)
        high = reduced.astype(bf16)
        low = (reduced - high.astype(f32)).astype(bf16)
        both = jnp.concatenate([high, low], axis=1)
        out_part = lax.dot_general(rank_twice, both, nt, preferred_element_type=f32)
        out_ref[i * sub : (i + 1) * sub, :] = in_part.astype(out_ref.dtype)
        for side in range(2):
            for piece in range(sub // lanes):
                row = tokens + side * stack + (i * (sub // lanes) + piece) * out_width
                out_ref[row : row + out_width, :] = out_part[
                    side * out_width : (side + 1) * out_width, piece * lanes : (piece + 1) * lanes
                ].astype(out_ref.dtype)


def project(mine, x, g, w, up, rank):
    tokens = x.shape[0] // 2
    sub = min(512, tokens)
    steps = tokens // sub
    depth = x.shape[1]
    rows = tokens + tokens // lanes * rank.shape[0]
    return pl.pallas_call(
        functools.partial(project_kernel, mine),
        in_specs=[pl.BlockSpec(memory_space=pltpu.HBM)] * 5,
        out_specs=pl.BlockSpec(memory_space=pltpu.VMEM),
        out_shape=jax.ShapeDtypeStruct((rows, lanes), f32 if mine else bf16),
        scratch_shapes=[
            pltpu.VMEM((steps, sub, depth), bf16),
            pltpu.VMEM((steps, sub, depth), bf16),
            pltpu.VMEM(w.shape, bf16),
            pltpu.VMEM(up.shape, bf16),
            pltpu.VMEM(rank.shape, bf16),
            pltpu.SemaphoreType.DMA((2 * steps + 3,)),
        ],
        compiler_params=params(16),
        cost_estimate=cost(4 * tokens * depth * lanes, 4 * tokens * depth),
        name="project",
    )(*(pltpu.with_memory_space_constraint(array, pltpu.HBM) for array in (x, g, w, up, rank)))


def square_kernel(targets_hbm, squares_ref, targets, sems):
    parts, rows, depth = targets.shape
    started = []
    for i in range(parts):
        part = pl.ds(i * rows, rows)
        started.append(pltpu.make_async_copy(targets_hbm.at[part, :], targets.at[i], sems.at[i]))
        started[-1].start()
    for i in range(parts):
        started[i].wait()
        totals = jnp.zeros((rows, lanes), f32)
        for k in range(depth // lanes):
            wide = targets[i, :, k * lanes : (k + 1) * lanes].astype(f32)
            totals += wide * wide
        squares_ref[:, i * rows : (i + 1) * rows] = jnp.sum(totals.T, axis=0, keepdims=True)


def row_squares(targets):
    columns, depth = targets.shape
    rows = min(256, columns)
    return pl.pallas_call(
        square_kernel,
        in_specs=[pl.BlockSpec(memory_space=pltpu.HBM)],
        out_specs=pl.BlockSpec(memory_space=pltpu.VMEM),
        out_shape=jax.ShapeDtypeStruct((1, columns), f32),
        scratch_shapes=[
            pltpu.VMEM((columns // rows, rows, depth), targets.dtype),
            pltpu.SemaphoreType.DMA((columns // rows,)),
        ],
        compiler_params=params(16),
        cost_estimate=cost(2 * columns * depth, 2 * columns * depth),
        name="squares",
    )(pltpu.with_memory_space_constraint(targets, pltpu.HBM))


def stage_kernel(targets_hbm, targets_ref, sem):
    copy = pltpu.make_async_copy(targets_hbm, targets_ref, sem)
    copy.start()
    copy.wait()


def stage(targets):
    return pl.pallas_call(
        stage_kernel,
        in_specs=[pl.BlockSpec(memory_space=pltpu.HBM)],
        out_specs=pl.BlockSpec(memory_space=pltpu.VMEM),
        out_shape=pltpu.VMEM(targets.shape, targets.dtype),
        scratch_shapes=[pltpu.SemaphoreType.DMA],
        compiler_params=params(12),
        cost_estimate=cost(0, 2 * targets.size),
        name="stage",
    )(pltpu.with_memory_space_constraint(targets, pltpu.HBM))


def core_sum_kernel(keep_ref, came_ref, send_ref, left_ref):
    rows = keep_ref.shape[0]
    final = send_ref.shape[0]
    stack = rows - final
    tokens = final - stack
    _, x = position()
    total = keep_ref[:tokens, :] + came_ref[:tokens, :].astype(f32)
    send_ref[:tokens, :] = total.astype(bf16)
    left_ref[:tokens, :] = total
    far = pl.ds(pl.multiple_of(tokens + (1 - x) * stack, stack), stack)
    near = pl.ds(pl.multiple_of(tokens + x * stack, stack), stack)
    send_ref[tokens:, :] = (keep_ref[far, :] + came_ref[far, :].astype(f32)).astype(bf16)
    left_ref[tokens:, :] = keep_ref[near, :] + came_ref[near, :].astype(f32)


def core_sum(keep, came, tokens):
    rows = keep.shape[0]
    final = tokens + (rows - tokens) // 2
    vmem = pl.BlockSpec(memory_space=pltpu.VMEM)
    return pl.pallas_call(
        core_sum_kernel,
        in_specs=[vmem, vmem],
        out_specs=[vmem, vmem],
        out_shape=[
            jax.ShapeDtypeStruct((final, lanes), bf16),
            jax.ShapeDtypeStruct((final, lanes), f32),
        ],
        compiler_params=params(8),
        cost_estimate=cost(rows * lanes, 12 * rows * lanes),
        name="core_sum",
    )(keep, came)


def feature_kernel(programs, lengths, left_ref, came_ref, mine_ref, other_ref, held):
    core, _ = position()
    quarter = mine_ref.shape[0]
    out_width = 2 * quarter
    final = left_ref.shape[0]
    tokens = final * lanes // (lanes + out_width)
    length = tokens // programs
    some = 8
    span = some * length
    program = lax.broadcasted_iota(jnp.int32, (some, span), 0)
    token = lax.broadcasted_iota(jnp.int32, (some, span), 1) - program * length
    for group in range(programs // some):
        rows = slice(group * span, (group + 1) * span)
        in_sum = (left_ref[rows, :] + came_ref[rows, :].astype(f32)).astype(bf16)
        first = tokens + group * (span // lanes) * out_width
        rows = slice(first, first + span // lanes * out_width)
        out_sum = left_ref[rows, :] + came_ref[rows, :].astype(f32)
        out_rows = jnp.concatenate(
            [out_sum[i * out_width : (i + 1) * out_width, :] for i in range(span // lanes)], axis=1
        )
        limit = jnp.zeros((some, span), jnp.int32)
        for s in range(some):
            limit = jnp.where(program == s, lengths[core * programs + group * some + s], limit)
        live = ((token >= 0) & (token < limit)).astype(f32)
        spread = (out_rows[:, None, :] * live[None, :, :]).reshape(out_width * some, span)
        made = jnp.dot(spread.astype(bf16), in_sum, preferred_element_type=f32)
        held[:, group * some : (group + 1) * some, :] = made.reshape(out_width, some, lanes)
    mine_ref[...] = held[pl.ds(core * quarter, quarter), :, :].astype(bf16)
    other_ref[...] = held[pl.ds((1 - core) * quarter, quarter), :, :].astype(bf16)


def make_features(programs, quarter, lengths, left, came):
    vmem = pl.BlockSpec(memory_space=pltpu.VMEM)
    shape = jax.ShapeDtypeStruct((quarter, programs, lanes), bf16)
    return pl.pallas_call(
        functools.partial(feature_kernel, programs),
        in_specs=[pl.BlockSpec(memory_space=pltpu.SMEM), vmem, vmem],
        out_specs=[vmem, vmem],
        out_shape=[shape, shape],
        scratch_shapes=[pltpu.VMEM((2 * quarter, programs, lanes), f32)],
        compiler_params=params(12),
        cost_estimate=cost(10**8, 8 * left.size),
        name="features",
    )(lengths, left, came)


def score_kernel(count, far, order_ref, targets_ref, *refs):
    pieces, sends, (keep_ref, ordered) = refs[:count], refs[count:-2], refs[-2:]
    columns, rows = targets_ref.shape[0], keep_ref.shape[0]

    def store(first, size, values):
        height = rows // len(sends)
        for i, ref in enumerate(sends):
            ref[:, first : first + size] = values[i * height : (i + 1) * height, :]
        keep_ref[:, first : first + size] = values[rows:, :]

    core, x = position()
    x = 1 - x if far else x
    position_rows = order_ref[...]
    row = lax.broadcasted_iota(jnp.int32, (2 * rows, position_rows.shape[1]), 0)
    first = jnp.where(row < rows, (x * 2 + 1 - core) * rows, (x * 2 + core) * rows - rows)
    chosen = (row + first == position_rows).astype(bf16)
    totals = jnp.zeros((2 * rows, lanes), f32)
    for a in range(0, pieces[0].shape[1], 2):
        block = jnp.concatenate(
            [
                jnp.concatenate([piece[i, a + d] for piece in pieces for i in range(2)], axis=0)
                for d in range(2)
            ],
            axis=1,
        )
        found = jnp.dot(chosen, block, preferred_element_type=f32)
        ordered[:, a * lanes : (a + 2) * lanes] = found.astype(bf16)
        totals += found[:, :lanes] * found[:, :lanes] + found[:, lanes:] * found[:, lanes:]
    store(columns, lanes, totals.astype(bf16))
    tile = min(512, columns)
    for j in range(0, columns, tile):
        scores = lax.dot_general(
            ordered[...], targets_ref[j : j + tile, :], nt, preferred_element_type=f32
        ).astype(bf16)
        store(j, tile, scores)


def partial_scores(far, order, pieces, targets, rows):
    columns, depth = targets.shape
    held = 2 * (4 * rows * depth + 4 * rows * columns + 8 * rows * order.size)
    limit = 6 + held // 1024**2
    vmem = pl.BlockSpec(memory_space=pltpu.VMEM)
    sends = 1 if far else 2
    shape = jax.ShapeDtypeStruct((rows // sends, columns + lanes), bf16)
    whole = jax.ShapeDtypeStruct((rows, columns + lanes), bf16)
    return pl.pallas_call(
        functools.partial(score_kernel, len(pieces), far),
        in_specs=[vmem] * (2 + len(pieces)),
        out_specs=[vmem] * (sends + 1),
        out_shape=[shape] * sends + [whole],
        scratch_shapes=[pltpu.VMEM((2 * rows, depth), bf16)],
        compiler_params=params(limit),
        cost_estimate=cost(4 * rows * columns * depth, 2 * columns * depth),
        name="scores_far" if far else "scores_near",
    )(order, pltpu.with_memory_space_constraint(targets, pltpu.VMEM), *pieces)


def join_kernel(keep_ref, came_ref, out_ref):
    out_ref[...] = (keep_ref[...].astype(f32) + came_ref[...].astype(f32)).astype(bf16)


def join(keep, came):
    vmem = pl.BlockSpec(memory_space=pltpu.VMEM)
    return pl.pallas_call(
        join_kernel,
        in_specs=[vmem, vmem],
        out_specs=vmem,
        out_shape=jax.ShapeDtypeStruct(keep.shape, bf16),
        compiler_params=params(16),
        cost_estimate=cost(keep.size, 6 * keep.size),
        name="join",
    )(keep, came)


def finish_kernel(root_count, keep_ref, low_ref, high_ref, far_ref, squares_ref, out_ref):
    columns = out_ref.shape[1]
    tile = min(512, columns)
    height = low_ref.shape[0]
    for i, near_ref in enumerate((low_ref, high_ref)):
        rows = slice(i * height, (i + 1) * height)

        def total(first, size):
            strip = slice(first, first + size)
            mine = keep_ref[rows, strip].astype(f32) + near_ref[:, strip].astype(f32)
            return mine + far_ref[rows, strip].astype(f32)

        squares = jnp.sum(total(columns, lanes), axis=1, keepdims=True)
        row_scale = lax.rsqrt(squares + epsilon) * root_count
        for j in range(0, columns, tile):
            column_scale = lax.rsqrt(squares_ref[:, j : j + tile] + epsilon)
            out_ref[rows, j : j + tile] = total(j, tile) * row_scale * column_scale


def finish(root_count, keep, low, high, far, squares):
    rows, columns = keep.shape[0], squares.shape[1]
    vmem = pl.BlockSpec(memory_space=pltpu.VMEM)
    return pl.pallas_call(
        functools.partial(finish_kernel, root_count),
        in_specs=[vmem] * 5,
        out_specs=vmem,
        out_shape=jax.ShapeDtypeStruct((rows, columns), f32),
        compiler_params=params(24),
        cost_estimate=cost(4 * rows * columns, 10 * rows * columns),
        name="finish",
    )(keep, low, high, far, squares)


def shards(
    layer_input_rows,
    output_gradient_rows,
    adapter_up_weight,
    input_side_projection,
    rank_side_projection,
    lengths,
    program_output_index,
    targets,
):
    wide_count, narrow_count = lax.axis_size("wide"), lax.axis_size("narrow")
    w, n = lax.axis_index("wide"), lax.axis_index("narrow")
    core, x = n % 2, n // 2
    programs = lengths.shape[0]
    length = layer_input_rows.shape[0] // programs
    quarter = rank_side_projection.shape[1] // narrow_count
    share = programs // 2
    tokens = share * length
    rank = rank_side_projection.T
    operands = (layer_input_rows, output_gradient_rows, input_side_projection, adapter_up_weight, rank)

    send = project(False, *operands)
    keep = project(True, *operands)
    send, left = core_sum(keep, exchange(send, "narrow", 1), tokens)
    squares = row_squares(after(targets, send))
    squares = squares + exchange(squares, "narrow", 1)
    squares = squares + exchange(squares, "narrow", 2)
    left, squares = lax.optimization_barrier((left, squares))
    came = exchange(send, "narrow", 2)
    mine, other = make_features(share, quarter, lengths, left, came)
    block = jnp.stack([mine, exchange(other, "narrow", 1)])
    pieces = gather_blocks(block)
    targets = stage(after(targets, pieces[-2]))

    order = program_output_index.reshape(wide_count, 2, share)
    order = jnp.take(order, w ^ jnp.arange(wide_count), axis=0)
    order = jnp.where(core == 1, order[:, ::-1], order).reshape(1, -1)
    rows = order.shape[1] // narrow_count

    far_send, far_keep = partial_scores(True, order, pieces, targets, rows)
    far = join(far_keep, exchange(far_send, "narrow", 1))
    order, far = lax.optimization_barrier((order, far))
    far = exchange(far, "narrow", 2)
    *near_sends, near_keep = partial_scores(False, order, pieces, targets, rows)
    near = [exchange(part, "narrow", 1) for part in near_sends]
    root_count = math.sqrt(float(targets.shape[1] * narrow_count))
    return finish(root_count, near_keep, *near, far, squares)


def solution(mesh):
    return jax.shard_map(
        shards,
        mesh=mesh,
        in_specs=(
            P("wide", "narrow"),
            P("wide", "narrow"),
            P("narrow", None),
            P("narrow", None),
            P(),
            P("wide"),
            P(),
            P("wide", "narrow"),
        ),
        out_specs=P("narrow", "wide"),
        check_vma=False,
    )
```

```python
import functools
import math

import jax
import jax.numpy as jnp
from jax import lax
from jax.experimental import pallas as pl
from jax.experimental.pallas import tpu as pltpu
from jax.sharding import PartitionSpec as P

epsilon = 1e-06
lanes = 128
chunks = 2
f32, bf16 = jnp.float32, jnp.bfloat16
nt = (((1,), (1,)), ((), ()))


def params(mebibytes):
    return pltpu.CompilerParams(vmem_limit_bytes=int(mebibytes * 1024 * 1024))


def cost(flops, moved):
    return pl.CostEstimate(flops=flops, bytes_accessed=moved, transcendentals=0)


def exchange(array, axis, bit):
    count = lax.axis_size(axis)
    return lax.ppermute(array, axis, [(i, i ^ bit) for i in range(count)])


def after(array, *others):
    return lax.optimization_barrier((array,) + others)[0]


def gather_blocks(blocks):
    count = lax.axis_size("wide")
    if count == 8 and chunks == 2:
        first, second = blocks
        far = [exchange(first, "wide", 4)]
        above = [exchange(first, "wide", 2)]
        beside = [exchange(first, "wide", 1)]
        second = after(second, far[0])
        far.append(exchange(second, "wide", 4))
        across = [exchange(far[0], "wide", 2)]
        far_beside = [exchange(after(far[0], beside[0], above[0]), "wide", 1)]
        beside.append(exchange(second, "wide", 1))
        above.append(exchange(second, "wide", 2))
        across.append(exchange(far[1], "wide", 2))
        far_beside.append(exchange(after(far[1], beside[1], above[1], far_beside[0]), "wide", 1))
        across_beside = [exchange(chunk, "wide", 1) for chunk in across]
        above_beside = [exchange(after(beside[i], across[i]), "wide", 2) for i in range(2)]
        return blocks, beside, above, above_beside, far, far_beside, across, across_beside
    held = {0: jnp.stack(blocks)}
    bit = count // 2
    while bit:
        for k in list(held):
            held[k | bit] = exchange(held[k], "wide", bit)
        bit //= 2
    return [[held[k]] for k in range(count)]


def position():
    n = lax.axis_index("narrow")
    return n % 2, n // 2


def project_kernel(mine, x_hbm, g_hbm, w_hbm, up_hbm, rank_hbm, out_ref, x, g, w, up, rank, sems):
    core, _ = position()
    half = core if mine else 1 - core
    steps, sub = x.shape[:2]
    tokens = steps * sub
    out_width = rank.shape[0] // 2
    stack = tokens // lanes * out_width

    def copies(i):
        rows = pl.ds(pl.multiple_of((half * steps + i) * sub, sub), sub)
        return [
            pltpu.make_async_copy(x_hbm.at[rows, :], x.at[i], sems.at[2 * i]),
            pltpu.make_async_copy(g_hbm.at[rows, :], g.at[i], sems.at[2 * i + 1]),
        ]

    weights = [
        pltpu.make_async_copy(w_hbm, w, sems.at[2 * steps]),
        pltpu.make_async_copy(up_hbm, up, sems.at[2 * steps + 1]),
        pltpu.make_async_copy(rank_hbm, rank, sems.at[2 * steps + 2]),
    ]
    started = [copies(i) for i in range(steps)]
    for copy in weights + [copy for pair in started for copy in pair]:
        copy.start()
    for copy in weights:
        copy.wait()
    rank_twice = jnp.concatenate([rank[...], rank[...]], axis=1)
    for i in range(steps):
        for copy in started[i]:
            copy.wait()
        in_part = jnp.dot(x[i], w[...], preferred_element_type=f32)
        reduced = jnp.dot(g[i], up[...], preferred_element_type=f32)
        high = reduced.astype(bf16)
        low = (reduced - high.astype(f32)).astype(bf16)
        both = jnp.concatenate([high, low], axis=1)
        out_part = lax.dot_general(rank_twice, both, nt, preferred_element_type=f32)
        out_ref[i * sub : (i + 1) * sub, :] = in_part.astype(out_ref.dtype)
        for side in range(2):
            for piece in range(sub // lanes):
                row = tokens + side * stack + (i * (sub // lanes) + piece) * out_width
                out_ref[row : row + out_width, :] = out_part[
                    side * out_width : (side + 1) * out_width, piece * lanes : (piece + 1) * lanes
                ].astype(out_ref.dtype)


def project(mine, x, g, w, up, rank):
    tokens = x.shape[0] // 2
    sub = min(512, tokens)
    steps = tokens // sub
    depth = x.shape[1]
    rows = tokens + tokens // lanes * rank.shape[0]
    return pl.pallas_call(
        functools.partial(project_kernel, mine),
        in_specs=[pl.BlockSpec(memory_space=pltpu.HBM)] * 5,
        out_specs=pl.BlockSpec(memory_space=pltpu.VMEM),
        out_shape=jax.ShapeDtypeStruct((rows, lanes), f32 if mine else bf16),
        scratch_shapes=[
            pltpu.VMEM((steps, sub, depth), bf16),
            pltpu.VMEM((steps, sub, depth), bf16),
            pltpu.VMEM(w.shape, bf16),
            pltpu.VMEM(up.shape, bf16),
            pltpu.VMEM(rank.shape, bf16),
            pltpu.SemaphoreType.DMA((2 * steps + 3,)),
        ],
        compiler_params=params(16),
        cost_estimate=cost(4 * tokens * depth * lanes, 4 * tokens * depth),
        name="project",
    )(*(pltpu.with_memory_space_constraint(array, pltpu.HBM) for array in (x, g, w, up, rank)))


def square_kernel(targets_hbm, squares_ref, targets, sems):
    parts, rows, depth = targets.shape
    started = []
    for i in range(parts):
        part = pl.ds(i * rows, rows)
        started.append(pltpu.make_async_copy(targets_hbm.at[part, :], targets.at[i], sems.at[i]))
        started[-1].start()
    for i in range(parts):
        started[i].wait()
        totals = jnp.zeros((rows, lanes), f32)
        for k in range(depth // lanes):
            wide = targets[i, :, k * lanes : (k + 1) * lanes].astype(f32)
            totals += wide * wide
        squares_ref[:, i * rows : (i + 1) * rows] = jnp.sum(totals.T, axis=0, keepdims=True)


def row_squares(targets):
    columns, depth = targets.shape
    rows = min(256, columns)
    return pl.pallas_call(
        square_kernel,
        in_specs=[pl.BlockSpec(memory_space=pltpu.HBM)],
        out_specs=pl.BlockSpec(memory_space=pltpu.VMEM),
        out_shape=jax.ShapeDtypeStruct((1, columns), f32),
        scratch_shapes=[
            pltpu.VMEM((columns // rows, rows, depth), targets.dtype),
            pltpu.SemaphoreType.DMA((columns // rows,)),
        ],
        compiler_params=params(16),
        cost_estimate=cost(2 * columns * depth, 2 * columns * depth),
        name="squares",
    )(pltpu.with_memory_space_constraint(targets, pltpu.HBM))


def stage_kernel(targets_hbm, targets_ref, sem):
    copy = pltpu.make_async_copy(targets_hbm, targets_ref, sem)
    copy.start()
    copy.wait()


def stage(targets):
    return pl.pallas_call(
        stage_kernel,
        in_specs=[pl.BlockSpec(memory_space=pltpu.HBM)],
        out_specs=pl.BlockSpec(memory_space=pltpu.VMEM),
        out_shape=pltpu.VMEM(targets.shape, targets.dtype),
        scratch_shapes=[pltpu.SemaphoreType.DMA],
        compiler_params=params(12),
        cost_estimate=cost(0, 2 * targets.size),
        name="stage",
    )(pltpu.with_memory_space_constraint(targets, pltpu.HBM))


def core_sum_kernel(keep_ref, came_ref, *outs):
    sends, lefts = outs[:chunks], outs[chunks:]
    rows = keep_ref.shape[0]
    final = sends[0].shape[0]
    stack = (rows - chunks * final) // chunks
    tokens = final - stack
    _, x = position()
    for i in range(chunks):
        part = slice(i * tokens, (i + 1) * tokens)
        total = keep_ref[part, :] + came_ref[part, :].astype(f32)
        sends[i][:tokens, :] = total.astype(bf16)
        lefts[i][:tokens, :] = total
        for side, ref in ((1 - x, sends[i]), (x, lefts[i])):
            first = chunks * tokens + (side * chunks + i) * stack
            part = pl.ds(pl.multiple_of(first, stack), stack)
            total = keep_ref[part, :] + came_ref[part, :].astype(f32)
            ref[tokens:, :] = total.astype(ref.dtype)


def core_sum(keep, came, tokens):
    rows = keep.shape[0]
    final = (tokens + (rows - tokens) // 2) // chunks
    vmem = pl.BlockSpec(memory_space=pltpu.VMEM)
    outs = pl.pallas_call(
        core_sum_kernel,
        in_specs=[vmem, vmem],
        out_specs=[vmem] * (2 * chunks),
        out_shape=[jax.ShapeDtypeStruct((final, lanes), dtype) for dtype in (bf16,) * chunks + (f32,) * chunks],
        compiler_params=params(8),
        cost_estimate=cost(rows * lanes, 12 * rows * lanes),
        name="core_sum",
    )(keep, came)
    return outs[:chunks], outs[chunks:]


def feature_kernel(chunk, programs, lengths, left_ref, came_ref, mine_ref, other_ref, held):
    core, _ = position()
    quarter = mine_ref.shape[0]
    out_width = 2 * quarter
    final = left_ref.shape[0]
    tokens = final * lanes // (lanes + out_width)
    length = tokens // programs
    some = 8
    span = some * length
    program = lax.broadcasted_iota(jnp.int32, (some, span), 0)
    token = lax.broadcasted_iota(jnp.int32, (some, span), 1) - program * length
    for group in range(programs // some):
        rows = slice(group * span, (group + 1) * span)
        in_sum = (left_ref[rows, :] + came_ref[rows, :].astype(f32)).astype(bf16)
        first = tokens + group * (span // lanes) * out_width
        rows = slice(first, first + span // lanes * out_width)
        out_sum = left_ref[rows, :] + came_ref[rows, :].astype(f32)
        out_rows = jnp.concatenate(
            [out_sum[i * out_width : (i + 1) * out_width, :] for i in range(span // lanes)], axis=1
        )
        limit = jnp.zeros((some, span), jnp.int32)
        for s in range(some):
            limit = jnp.where(program == s, lengths[(core * chunks + chunk) * programs + group * some + s], limit)
        live = ((token >= 0) & (token < limit)).astype(f32)
        spread = (out_rows[:, None, :] * live[None, :, :]).reshape(out_width * some, span)
        made = jnp.dot(spread.astype(bf16), in_sum, preferred_element_type=f32)
        held[:, group * some : (group + 1) * some, :] = made.reshape(out_width, some, lanes)
    mine_ref[...] = held[pl.ds(core * quarter, quarter), :, :].astype(bf16)
    other_ref[...] = held[pl.ds((1 - core) * quarter, quarter), :, :].astype(bf16)


def make_features(chunk, programs, quarter, lengths, left, came):
    vmem = pl.BlockSpec(memory_space=pltpu.VMEM)
    shape = jax.ShapeDtypeStruct((quarter, programs, lanes), bf16)
    return pl.pallas_call(
        functools.partial(feature_kernel, chunk, programs),
        in_specs=[pl.BlockSpec(memory_space=pltpu.SMEM), vmem, vmem],
        out_specs=[vmem, vmem],
        out_shape=[shape, shape],
        scratch_shapes=[pltpu.VMEM((2 * quarter, programs, lanes), f32)],
        compiler_params=params(12),
        cost_estimate=cost(10**8, 8 * left.size),
        name="features",
    )(lengths, left, came)


def score_kernel(count, far, order_ref, targets_ref, *refs):
    pieces, sends, (keep_ref, ordered) = refs[:count], refs[count:-2], refs[-2:]
    columns, rows = targets_ref.shape[0], keep_ref.shape[0]

    def store(first, size, values):
        height = rows // len(sends)
        for i, ref in enumerate(sends):
            ref[:, first : first + size] = values[i * height : (i + 1) * height, :]
        keep_ref[:, first : first + size] = values[rows:, :]

    core, x = position()
    x = 1 - x if far else x
    position_rows = order_ref[...]
    row = lax.broadcasted_iota(jnp.int32, (2 * rows, position_rows.shape[1]), 0)
    first = jnp.where(row < rows, (x * 2 + 1 - core) * rows, (x * 2 + core) * rows - rows)
    chosen = (row + first == position_rows).astype(bf16)
    totals = jnp.zeros((2 * rows, lanes), f32)
    halves = pieces
    while any(ref.ndim > 3 for ref in halves):
        halves = [half for ref in halves for half in ([ref.at[i] for i in range(ref.shape[0])] if ref.ndim > 3 else [ref])]
    for a in range(0, halves[0].shape[0], 2):
        block = jnp.concatenate(
            [
                jnp.concatenate([half[a + d] for half in halves], axis=0)
                for d in range(2)
            ],
            axis=1,
        )
        found = jnp.dot(chosen, block, preferred_element_type=f32)
        ordered[:, a * lanes : (a + 2) * lanes] = found.astype(bf16)
        totals += found[:, :lanes] * found[:, :lanes] + found[:, lanes:] * found[:, lanes:]
    store(columns, lanes, totals.astype(bf16))
    tile = min(512, columns)
    for j in range(0, columns, tile):
        scores = lax.dot_general(
            ordered[...], targets_ref[j : j + tile, :], nt, preferred_element_type=f32
        ).astype(bf16)
        store(j, tile, scores)


def partial_scores(far, order, pieces, targets, rows):
    columns, depth = targets.shape
    held = 2 * (4 * rows * depth + 4 * rows * columns + 8 * rows * order.size)
    limit = 6 + held // 1024**2
    vmem = pl.BlockSpec(memory_space=pltpu.VMEM)
    sends = 1 if far else 2
    shape = jax.ShapeDtypeStruct((rows // sends, columns + lanes), bf16)
    whole = jax.ShapeDtypeStruct((rows, columns + lanes), bf16)
    return pl.pallas_call(
        functools.partial(score_kernel, len(pieces), far),
        in_specs=[vmem] * (2 + len(pieces)),
        out_specs=[vmem] * (sends + 1),
        out_shape=[shape] * sends + [whole],
        scratch_shapes=[pltpu.VMEM((2 * rows, depth), bf16)],
        compiler_params=params(limit),
        cost_estimate=cost(4 * rows * columns * depth, 2 * columns * depth),
        name="scores_far" if far else "scores_near",
    )(order, pltpu.with_memory_space_constraint(targets, pltpu.VMEM), *pieces)


def join_kernel(keep_ref, came_ref, out_ref):
    out_ref[...] = (keep_ref[...].astype(f32) + came_ref[...].astype(f32)).astype(bf16)


def join(keep, came):
    vmem = pl.BlockSpec(memory_space=pltpu.VMEM)
    return pl.pallas_call(
        join_kernel,
        in_specs=[vmem, vmem],
        out_specs=vmem,
        out_shape=jax.ShapeDtypeStruct(keep.shape, bf16),
        compiler_params=params(16),
        cost_estimate=cost(keep.size, 6 * keep.size),
        name="join",
    )(keep, came)


def finish_kernel(root_count, keep_ref, low_ref, high_ref, far_ref, squares_ref, out_ref):
    columns = out_ref.shape[1]
    tile = min(512, columns)
    height = low_ref.shape[0]
    for i, near_ref in enumerate((low_ref, high_ref)):
        rows = slice(i * height, (i + 1) * height)

        def total(first, size):
            strip = slice(first, first + size)
            mine = keep_ref[rows, strip].astype(f32) + near_ref[:, strip].astype(f32)
            return mine + far_ref[rows, strip].astype(f32)

        squares = jnp.sum(total(columns, lanes), axis=1, keepdims=True)
        row_scale = lax.rsqrt(squares + epsilon) * root_count
        for j in range(0, columns, tile):
            column_scale = lax.rsqrt(squares_ref[:, j : j + tile] + epsilon)
            out_ref[rows, j : j + tile] = total(j, tile) * row_scale * column_scale


def finish(root_count, keep, low, high, far, squares):
    rows, columns = keep.shape[0], squares.shape[1]
    vmem = pl.BlockSpec(memory_space=pltpu.VMEM)
    return pl.pallas_call(
        functools.partial(finish_kernel, root_count),
        in_specs=[vmem] * 5,
        out_specs=vmem,
        out_shape=jax.ShapeDtypeStruct((rows, columns), f32),
        compiler_params=params(24),
        cost_estimate=cost(4 * rows * columns, 10 * rows * columns),
        name="finish",
    )(keep, low, high, far, squares)


def shards(
    layer_input_rows,
    output_gradient_rows,
    adapter_up_weight,
    input_side_projection,
    rank_side_projection,
    lengths,
    program_output_index,
    targets,
):
    wide_count, narrow_count = lax.axis_size("wide"), lax.axis_size("narrow")
    w, n = lax.axis_index("wide"), lax.axis_index("narrow")
    core, x = n % 2, n // 2
    programs = lengths.shape[0]
    length = layer_input_rows.shape[0] // programs
    quarter = rank_side_projection.shape[1] // narrow_count
    share = programs // 2
    tokens = share * length
    rank = rank_side_projection.T
    operands = (layer_input_rows, output_gradient_rows, input_side_projection, adapter_up_weight, rank)

    send = project(False, *operands)
    keep = project(True, *operands)
    sends, lefts = core_sum(keep, exchange(send, "narrow", 1), tokens)
    squares = row_squares(after(targets, sends[0]))
    squares = squares + exchange(squares, "narrow", 1)
    squares = squares + exchange(squares, "narrow", 2)
    blocks = []
    for i in range(chunks):
        came = exchange(sends[i], "narrow", 2)
        left = after(lefts[i], *blocks) if blocks else lefts[i]
        mine, other = make_features(i, share // chunks, quarter, lengths, left, came)
        blocks.append(jnp.stack([mine, exchange(other, "narrow", 1)]))
    pieces = gather_blocks(blocks)
    targets = stage(after(targets, pieces[-2][-1]))
    pieces = [chunk for piece in pieces for chunk in piece]

    order = program_output_index.reshape(wide_count, 2, chunks, share // chunks)
    order = jnp.take(order, w ^ jnp.arange(wide_count), axis=0)
    order = jnp.where(core == 1, order[:, ::-1], order).transpose(0, 2, 1, 3).reshape(1, -1)
    rows = order.shape[1] // narrow_count

    far_send, far_keep = partial_scores(True, order, pieces, targets, rows)
    far = join(far_keep, exchange(far_send, "narrow", 1))
    order, far = lax.optimization_barrier((order, far))
    far = exchange(far, "narrow", 2)
    *near_sends, near_keep = partial_scores(False, order, pieces, targets, rows)
    near = [exchange(part, "narrow", 1) for part in near_sends]
    root_count = math.sqrt(float(targets.shape[1] * narrow_count))
    return finish(root_count, near_keep, *near, far, squares)


def solution(mesh):
    return jax.shard_map(
        shards,
        mesh=mesh,
        in_specs=(
            P("wide", "narrow"),
            P("wide", "narrow"),
            P("narrow", None),
            P("narrow", None),
            P(),
            P("wide"),
            P(),
            P("wide", "narrow"),
        ),
        out_specs=P("narrow", "wide"),
        check_vma=False,
    )
```

```python
import functools
import math

import jax
import jax.numpy as jnp
from jax import lax
from jax.experimental import pallas as pl
from jax.experimental.pallas import tpu as pltpu
from jax.sharding import PartitionSpec as P

epsilon = 1e-06
lanes = 128
chunks = 2
middle = lanes // 2
f32, bf16 = jnp.float32, jnp.bfloat16
nt = (((1,), (1,)), ((), ()))


def params(mebibytes):
    return pltpu.CompilerParams(vmem_limit_bytes=int(mebibytes * 1024 * 1024))


def cost(flops, moved):
    return pl.CostEstimate(flops=flops, bytes_accessed=moved, transcendentals=0)


def exchange(array, axis, bit):
    count = lax.axis_size(axis)
    return lax.ppermute(array, axis, [(i, i ^ bit) for i in range(count)])


def after(array, *others):
    return lax.optimization_barrier((array,) + others)[0]


def gather_blocks(blocks):
    count = lax.axis_size("wide")
    if count == 8 and chunks == 2:
        first, second = blocks
        far = [exchange(first, "wide", 4)]
        above = [exchange(first, "wide", 2)]
        beside = [exchange(first, "wide", 1)]
        second = after(second, far[0])
        far.append(exchange(second, "wide", 4))
        across = [exchange(far[0], "wide", 2)]
        far_beside = [exchange(after(far[0], beside[0], above[0]), "wide", 1)]
        beside.append(exchange(second, "wide", 1))
        above.append(exchange(second, "wide", 2))
        across.append(exchange(far[1], "wide", 2))
        far_beside.append(exchange(after(far[1], beside[1], above[1]), "wide", 1))
        across_beside = [exchange(chunk, "wide", 1) for chunk in across]
        above_beside = [exchange(after(beside[0], across[0]), "wide", 2), exchange(after(beside[1], across[1]), "wide", 2)]
        return blocks, beside, above, above_beside, far, far_beside, across, across_beside
    held = {0: jnp.stack(blocks)}
    bit = count // 2
    while bit:
        for k in list(held):
            held[k | bit] = exchange(held[k], "wide", bit)
        bit //= 2
    return [[held[k]] for k in range(count)]


def position():
    n = lax.axis_index("narrow")
    return n % 2, n // 2


def project_rows(x, g, w, up, rank_twice, out_ref, i, tokens):
    sub = x.shape[0]
    out_width = rank_twice.shape[0] // 2
    stack = tokens // lanes * out_width
    in_part = jnp.dot(x, w, preferred_element_type=f32)
    reduced = jnp.dot(g, up, preferred_element_type=f32)
    high = reduced.astype(bf16)
    low = (reduced - high.astype(f32)).astype(bf16)
    both = jnp.concatenate([high, low], axis=1)
    out_part = lax.dot_general(rank_twice, both, nt, preferred_element_type=f32)
    out_ref[i * sub : (i + 1) * sub, :] = in_part.astype(out_ref.dtype)
    for side in range(2):
        for piece in range(sub // lanes):
            row = tokens + side * stack + (i * (sub // lanes) + piece) * out_width
            out_ref[row : row + out_width, :] = out_part[
                side * out_width : (side + 1) * out_width, piece * lanes : (piece + 1) * lanes
            ].astype(out_ref.dtype)


def project_send_kernel(
    x_hbm, g_hbm, w_hbm, up_hbm, rank_hbm, out_ref, x_mine, g_mine, w, up, x, g, rank, sems
):
    core, _ = position()
    steps, sub = x.shape[:2]
    tokens = steps * sub

    def rows(half, i):
        return pl.ds(pl.multiple_of((half * steps + i) * sub, sub), sub)

    started = [
        pltpu.make_async_copy(w_hbm, w, sems.at[0]),
        pltpu.make_async_copy(up_hbm, up, sems.at[1]),
        pltpu.make_async_copy(rank_hbm, rank, sems.at[2]),
    ]
    for i in range(steps):
        part = rows(1 - core, i)
        started.append(pltpu.make_async_copy(x_hbm.at[part, :], x.at[i], sems.at[len(started)]))
        started.append(pltpu.make_async_copy(g_hbm.at[part, :], g.at[i], sems.at[len(started)]))
    part = pl.ds(pl.multiple_of(core * tokens, tokens), tokens)
    started.append(pltpu.make_async_copy(x_hbm.at[part, :], x_mine, sems.at[len(started)]))
    started.append(pltpu.make_async_copy(g_hbm.at[part, :], g_mine, sems.at[len(started)]))
    for copy in started:
        copy.start()
    for copy in started[:3]:
        copy.wait()
    rank_twice = jnp.concatenate([rank[...], rank[...]], axis=1)
    for i in range(steps):
        started[3 + 2 * i].wait()
        started[4 + 2 * i].wait()
        project_rows(x[i], g[i], w[...], up[...], rank_twice, out_ref, i, tokens)
    started[-2].wait()
    started[-1].wait()


def project_keep_kernel(x, g, w, up, rank, out_ref):
    rank_twice = jnp.concatenate([rank[...], rank[...]], axis=1)
    tokens = x.shape[0]
    sub = min(512, tokens)
    for i in range(tokens // sub):
        part = slice(i * sub, (i + 1) * sub)
        project_rows(x[part, :], g[part, :], w[...], up[...], rank_twice, out_ref, i, tokens)


def project_send(x, g, w, up, rank):
    tokens, depth = x.shape[0] // 2, x.shape[1]
    sub = min(512, tokens)
    steps = tokens // sub
    rows = tokens + tokens // lanes * rank.shape[0]
    vmem = pl.BlockSpec(memory_space=pltpu.VMEM)
    return pl.pallas_call(
        project_send_kernel,
        in_specs=[pl.BlockSpec(memory_space=pltpu.HBM)] * 5,
        out_specs=[vmem] * 5,
        out_shape=[
            jax.ShapeDtypeStruct((rows, lanes), bf16),
            pltpu.VMEM((tokens, depth), bf16),
            pltpu.VMEM((tokens, depth), bf16),
            pltpu.VMEM(w.shape, bf16),
            pltpu.VMEM(up.shape, bf16),
        ],
        scratch_shapes=[
            pltpu.VMEM((steps, sub, depth), bf16),
            pltpu.VMEM((steps, sub, depth), bf16),
            pltpu.VMEM(rank.shape, bf16),
            pltpu.SemaphoreType.DMA((2 * steps + 5,)),
        ],
        compiler_params=params(24),
        cost_estimate=cost(4 * tokens * depth * lanes, 8 * tokens * depth),
        name="project_send",
    )(*(pltpu.with_memory_space_constraint(array, pltpu.HBM) for array in (x, g, w, up, rank)))


def project_keep(x, g, w, up, rank):
    tokens, depth = x.shape
    rows = tokens + tokens // lanes * rank.shape[0]
    vmem = pl.BlockSpec(memory_space=pltpu.VMEM)
    return pl.pallas_call(
        project_keep_kernel,
        in_specs=[vmem] * 5,
        out_specs=vmem,
        out_shape=jax.ShapeDtypeStruct((rows, lanes), f32),
        compiler_params=params(16),
        cost_estimate=cost(4 * tokens * depth * lanes, 4 * tokens * depth),
        name="project_keep",
    )(*(pltpu.with_memory_space_constraint(array, pltpu.VMEM) for array in (x, g, w, up)), rank)


def square_kernel(targets_hbm, squares_ref, targets, sems):
    parts, rows, depth = targets.shape
    started = []
    for i in range(parts):
        part = pl.ds(i * rows, rows)
        started.append(pltpu.make_async_copy(targets_hbm.at[part, :], targets.at[i], sems.at[i]))
        started[-1].start()
    lane = lax.broadcasted_iota(jnp.int32, (lanes, lanes), 1)
    squares = jnp.zeros((lanes, lanes), f32)
    for i in range(parts):
        started[i].wait()
        for first in range(0, rows, lanes):
            totals = jnp.zeros((lanes, lanes), f32)
            for k in range(depth // lanes):
                wide = targets[i, first : first + lanes, k * lanes : (k + 1) * lanes].astype(f32)
                totals += wide * wide
            total = jnp.sum(totals, axis=1, keepdims=True)
            squares = jnp.where(lane == (i * rows + first) // lanes, total, squares)
    squares_ref[...] = squares


def column_squares(targets):
    columns, depth = targets.shape
    rows = min(256, columns)
    return pl.pallas_call(
        square_kernel,
        in_specs=[pl.BlockSpec(memory_space=pltpu.HBM)],
        out_specs=pl.BlockSpec(memory_space=pltpu.VMEM),
        out_shape=jax.ShapeDtypeStruct((lanes, lanes), f32),
        scratch_shapes=[
            pltpu.VMEM((columns // rows, rows, depth), targets.dtype),
            pltpu.SemaphoreType.DMA((columns // rows,)),
        ],
        compiler_params=params(16),
        cost_estimate=cost(2 * columns * depth, 2 * columns * depth),
        name="squares",
    )(pltpu.with_memory_space_constraint(targets, pltpu.HBM))


def stage_kernel(targets_hbm, targets_ref, sem):
    copy = pltpu.make_async_copy(targets_hbm, targets_ref, sem)
    copy.start()
    copy.wait()


def stage(targets):
    return pl.pallas_call(
        stage_kernel,
        in_specs=[pl.BlockSpec(memory_space=pltpu.HBM)],
        out_specs=pl.BlockSpec(memory_space=pltpu.VMEM),
        out_shape=pltpu.VMEM(targets.shape, targets.dtype),
        scratch_shapes=[pltpu.SemaphoreType.DMA],
        compiler_params=params(12),
        cost_estimate=cost(0, 2 * targets.size),
        name="stage",
    )(pltpu.with_memory_space_constraint(targets, pltpu.HBM))


def core_sum_kernel(keep_ref, came_ref, *outs):
    sends, lefts = outs[:chunks], outs[chunks:]
    rows = keep_ref.shape[0]
    final = sends[0].shape[0]
    stack = (rows - chunks * final) // chunks
    tokens = final - stack
    _, x = position()
    for i in range(chunks):
        part = slice(i * tokens, (i + 1) * tokens)
        total = keep_ref[part, :] + came_ref[part, :].astype(f32)
        sends[i][:tokens, :] = total.astype(bf16)
        lefts[i][:tokens, :] = total
        for side, ref in ((1 - x, sends[i]), (x, lefts[i])):
            first = chunks * tokens + (side * chunks + i) * stack
            part = pl.ds(pl.multiple_of(first, stack), stack)
            total = keep_ref[part, :] + came_ref[part, :].astype(f32)
            ref[tokens:, :] = total.astype(ref.dtype)


def core_sum(keep, came, tokens):
    rows = keep.shape[0]
    final = (tokens + (rows - tokens) // 2) // chunks
    vmem = pl.BlockSpec(memory_space=pltpu.VMEM)
    outs = pl.pallas_call(
        core_sum_kernel,
        in_specs=[vmem, vmem],
        out_specs=[vmem] * (2 * chunks),
        out_shape=[jax.ShapeDtypeStruct((final, lanes), dtype) for dtype in (bf16,) * chunks + (f32,) * chunks],
        compiler_params=params(8),
        cost_estimate=cost(rows * lanes, 12 * rows * lanes),
        name="core_sum",
    )(keep, came)
    return list(outs[:chunks]), list(outs[chunks:])


def feature_kernel(chunk, programs, lengths, left_ref, came_ref, mine_ref, other_ref, held):
    core, _ = position()
    quarter = mine_ref.shape[0]
    out_width = 2 * quarter
    final = left_ref.shape[0]
    tokens = final * lanes // (lanes + out_width)
    length = tokens // programs
    some = 8
    span = some * length
    program = lax.broadcasted_iota(jnp.int32, (some, span), 0)
    token = lax.broadcasted_iota(jnp.int32, (some, span), 1) - program * length
    for group in range(programs // some):
        rows = slice(group * span, (group + 1) * span)
        in_sum = (left_ref[rows, :] + came_ref[rows, :].astype(f32)).astype(bf16)
        first = tokens + group * (span // lanes) * out_width
        rows = slice(first, first + span // lanes * out_width)
        out_sum = left_ref[rows, :] + came_ref[rows, :].astype(f32)
        out_rows = jnp.concatenate(
            [out_sum[i * out_width : (i + 1) * out_width, :] for i in range(span // lanes)], axis=1
        )
        limit = jnp.zeros((some, span), jnp.int32)
        for s in range(some):
            limit = jnp.where(program == s, lengths[(core * chunks + chunk) * programs + group * some + s], limit)
        live = ((token >= 0) & (token < limit)).astype(f32)
        spread = (out_rows[:, None, :] * live[None, :, :]).reshape(out_width * some, span)
        made = jnp.dot(spread.astype(bf16), in_sum, preferred_element_type=f32)
        held[:, group * some : (group + 1) * some, :] = made.reshape(out_width, some, lanes)
    mine_ref[...] = held[pl.ds(core * quarter, quarter), :, :].astype(bf16)
    other_ref[...] = held[pl.ds((1 - core) * quarter, quarter), :, :].astype(bf16)


def make_features(chunk, programs, quarter, lengths, left, came):
    vmem = pl.BlockSpec(memory_space=pltpu.VMEM)
    shape = jax.ShapeDtypeStruct((quarter, programs, lanes), bf16)
    return pl.pallas_call(
        functools.partial(feature_kernel, chunk, programs),
        in_specs=[pl.BlockSpec(memory_space=pltpu.SMEM), vmem, vmem],
        out_specs=[vmem, vmem],
        out_shape=[shape, shape],
        scratch_shapes=[pltpu.VMEM((2 * quarter, programs, lanes), f32)],
        compiler_params=params(12),
        cost_estimate=cost(10**8, 8 * left.size),
        name="features",
    )(lengths, left, came)


def score_kernel(count, far, order_ref, squares_ref, targets_ref, *refs):
    pieces, sends, (keep_ref, ordered) = refs[:count], refs[count:-2], refs[-2:]
    columns, rows = targets_ref.shape[0], keep_ref.shape[0]

    def store(first, size, values):
        height = rows // len(sends)
        for i, ref in enumerate(sends):
            ref[:, first : first + size] = values[i * height : (i + 1) * height, :]
        keep_ref[:, first : first + size] = values[rows:, :]

    core, x = position()
    x = 1 - x if far else x
    position_rows = order_ref[...]
    row = lax.broadcasted_iota(jnp.int32, (2 * rows, position_rows.shape[1]), 0)
    first = jnp.where(row < rows, (x * 2 + 1 - core) * rows, (x * 2 + core) * rows - rows)
    chosen = (row + first == position_rows).astype(bf16)
    totals = jnp.zeros((2 * rows, lanes), f32)
    halves = pieces
    while any(ref.ndim > 3 for ref in halves):
        halves = [half for ref in halves for half in ([ref.at[i] for i in range(ref.shape[0])] if ref.ndim > 3 else [ref])]
    for a in range(0, halves[0].shape[0], 2):
        block = jnp.concatenate(
            [
                jnp.concatenate([half[a + d] for half in halves], axis=0)
                for d in range(2)
            ],
            axis=1,
        )
        found = jnp.dot(chosen, block, preferred_element_type=f32)
        ordered[:, a * lanes : (a + 2) * lanes] = found.astype(bf16)
        totals += found[:, :lanes] * found[:, :lanes] + found[:, lanes:] * found[:, lanes:]
    lane = lax.broadcasted_iota(jnp.int32, (2 * rows, lanes), 1)
    row_squares = jnp.sum(totals, axis=1, keepdims=True)
    spare = jnp.zeros((rows - lanes, lanes), f32)
    squares = jnp.concatenate([squares_ref[...], spare] * 2 if rows > lanes else [squares_ref[...]] * 2, axis=0)
    store(columns, lanes, jnp.where(lane == middle, row_squares, squares).astype(bf16))
    tile = min(512, columns)
    for j in range(0, columns, tile):
        scores = lax.dot_general(
            ordered[...], targets_ref[j : j + tile, :], nt, preferred_element_type=f32
        ).astype(bf16)
        store(j, tile, scores)


def partial_scores(far, order, squares, pieces, targets, rows):
    columns, depth = targets.shape
    held = 2 * (4 * rows * depth + 4 * rows * columns + 8 * rows * order.size)
    limit = 6 + held // 1024**2
    vmem = pl.BlockSpec(memory_space=pltpu.VMEM)
    sends = 1 if far else 2
    shape = jax.ShapeDtypeStruct((rows // sends, columns + lanes), bf16)
    whole = jax.ShapeDtypeStruct((rows, columns + lanes), bf16)
    return pl.pallas_call(
        functools.partial(score_kernel, len(pieces), far),
        in_specs=[vmem] * (3 + len(pieces)),
        out_specs=[vmem] * (sends + 1),
        out_shape=[shape] * sends + [whole],
        scratch_shapes=[pltpu.VMEM((2 * rows, depth), bf16)],
        compiler_params=params(limit),
        cost_estimate=cost(4 * rows * columns * depth, 2 * columns * depth),
        name="scores_far" if far else "scores_near",
    )(order, squares, pltpu.with_memory_space_constraint(targets, pltpu.VMEM), *pieces)


def join_kernel(keep_ref, came_ref, out_ref):
    out_ref[...] = (keep_ref[...].astype(f32) + came_ref[...].astype(f32)).astype(bf16)


def join(keep, came):
    vmem = pl.BlockSpec(memory_space=pltpu.VMEM)
    return pl.pallas_call(
        join_kernel,
        in_specs=[vmem, vmem],
        out_specs=vmem,
        out_shape=jax.ShapeDtypeStruct(keep.shape, bf16),
        compiler_params=params(16),
        cost_estimate=cost(keep.size, 6 * keep.size),
        name="join",
    )(keep, came)


def finish_kernel(root_count, keep_ref, low_ref, high_ref, far_ref, out_ref):
    columns = out_ref.shape[1]
    height = low_ref.shape[0]

    def total(i, first, size):
        rows, strip = slice(i * height, (i + 1) * height), slice(first, first + size)
        mine = keep_ref[rows, strip].astype(f32) + (low_ref, high_ref)[i][:, strip].astype(f32)
        return mine + far_ref[rows, strip].astype(f32)

    squares = jnp.concatenate([total(i, columns, lanes) for i in range(2)], axis=0)
    row_scale = lax.rsqrt(squares[:, middle : middle + 1] + epsilon) * root_count
    column_scale = lax.rsqrt(squares[:lanes, :].T + epsilon)
    for i in range(2):
        rows = slice(i * height, (i + 1) * height)
        for q in range(columns // lanes):
            scaled = total(i, q * lanes, lanes) * row_scale[rows, :] * column_scale[q : q + 1, :]
            out_ref[rows, q * lanes : (q + 1) * lanes] = scaled


def finish(root_count, keep, low, high, far):
    rows, columns = keep.shape[0], keep.shape[1] - lanes
    vmem = pl.BlockSpec(memory_space=pltpu.VMEM)
    return pl.pallas_call(
        functools.partial(finish_kernel, root_count),
        in_specs=[vmem] * 4,
        out_specs=vmem,
        out_shape=jax.ShapeDtypeStruct((rows, columns), f32),
        compiler_params=params(24),
        cost_estimate=cost(4 * rows * columns, 10 * rows * columns),
        name="finish",
    )(keep, low, high, far)


def shards(
    layer_input_rows,
    output_gradient_rows,
    adapter_up_weight,
    input_side_projection,
    rank_side_projection,
    lengths,
    program_output_index,
    targets,
):
    wide_count, narrow_count = lax.axis_size("wide"), lax.axis_size("narrow")
    w, n = lax.axis_index("wide"), lax.axis_index("narrow")
    core, x = n % 2, n // 2
    programs = lengths.shape[0]
    length = layer_input_rows.shape[0] // programs
    quarter = rank_side_projection.shape[1] // narrow_count
    share = programs // 2
    tokens = share * length
    rank = rank_side_projection.T
    send, *staged = project_send(
        layer_input_rows, output_gradient_rows, input_side_projection, adapter_up_weight, rank
    )
    keep = project_keep(*staged, rank)
    sends, lefts = core_sum(keep, exchange(send, "narrow", 1), tokens)
    squares = column_squares(after(targets, sends[0]))
    lefts[0], squares = lax.optimization_barrier((lefts[0], squares))
    blocks = []
    for i in range(chunks):
        came = exchange(sends[i], "narrow", 2)
        left = after(lefts[i], *blocks) if blocks else lefts[i]
        mine, other = make_features(i, share // chunks, quarter, lengths, left, came)
        blocks.append(jnp.stack([mine, exchange(other, "narrow", 1)]))
    pieces = gather_blocks(blocks)
    targets = stage(after(targets, pieces[-2][-1]))
    pieces = [chunk for piece in pieces for chunk in piece]

    order = program_output_index.reshape(wide_count, 2, chunks, share // chunks)
    order = jnp.take(order, w ^ jnp.arange(wide_count), axis=0)
    order = jnp.where(core == 1, order[:, ::-1], order).transpose(0, 2, 1, 3).reshape(1, -1)
    rows = order.shape[1] // narrow_count

    far_send, far_keep = partial_scores(True, order, squares, pieces, targets, rows)
    far = join(far_keep, exchange(far_send, "narrow", 1))
    order, far = lax.optimization_barrier((order, far))
    far = exchange(far, "narrow", 2)
    *near_sends, near_keep = partial_scores(False, order, squares, pieces, targets, rows)
    near = [exchange(part, "narrow", 1) for part in near_sends]
    root_count = math.sqrt(float(targets.shape[1] * narrow_count))
    return finish(root_count, near_keep, *near, far)


def solution(mesh):
    return jax.shard_map(
        shards,
        mesh=mesh,
        in_specs=(
            P("wide", "narrow"),
            P("wide", "narrow"),
            P("narrow", None),
            P("narrow", None),
            P(),
            P("wide"),
            P(),
            P("wide", "narrow"),
        ),
        out_specs=P("narrow", "wide"),
        check_vma=False,
    )
```

```python
import functools
import math

import jax
import jax.numpy as jnp
from jax import lax
from jax.experimental import pallas as pl
from jax.experimental.pallas import tpu as pltpu
from jax.sharding import PartitionSpec as P

epsilon = 1e-06
lanes = 128
chunks = 2
middle = lanes // 2
f32, bf16 = jnp.float32, jnp.bfloat16
nt = (((1,), (1,)), ((), ()))


def params(mebibytes):
    return pltpu.CompilerParams(vmem_limit_bytes=int(mebibytes * 1024 * 1024))


def cost(flops, moved):
    return pl.CostEstimate(flops=flops, bytes_accessed=moved, transcendentals=0)


def exchange(array, axis, bit):
    count = lax.axis_size(axis)
    return lax.ppermute(array, axis, [(i, i ^ bit) for i in range(count)])


def after(array, *others):
    return lax.optimization_barrier((array,) + others)[0]


def gather_blocks(blocks):
    count = lax.axis_size("wide")
    if count == 8 and chunks == 2:
        first, second = blocks
        far = [exchange(first, "wide", 4)]
        above = [exchange(first, "wide", 2)]
        beside = [exchange(first, "wide", 1)]
        second = after(second, far[0])
        far.append(exchange(second, "wide", 4))
        across = [exchange(far[0], "wide", 2)]
        far_beside = [exchange(after(far[0], beside[0], above[0]), "wide", 1)]
        beside.append(exchange(second, "wide", 1))
        above.append(exchange(second, "wide", 2))
        across.append(exchange(far[1], "wide", 2))
        far_beside.append(exchange(after(far[1], beside[1], above[1]), "wide", 1))
        across_beside = [exchange(chunk, "wide", 1) for chunk in across]
        above_beside = [exchange(after(beside[0], across[0]), "wide", 2), exchange(after(beside[1], across[1]), "wide", 2)]
        return blocks, beside, above, above_beside, far, far_beside, across, across_beside
    held = {0: blocks}
    bit = count // 2
    while bit:
        for k in list(held):
            held[k | bit] = [exchange(chunk, "wide", bit) for chunk in held[k]]
        bit //= 2
    return [held[k] for k in range(count)]


def parts_of(programs):
    number = programs // chunks
    return [(i * number, number) for i in range(chunks)]


def position():
    n = lax.axis_index("narrow")
    return n % 2, n // 2


def project_rows(x, g, w, up, rank_twice, out_ref, i, tokens):
    sub = x.shape[0]
    out_width = rank_twice.shape[0] // 2
    stack = tokens // lanes * out_width
    in_part = jnp.dot(x, w, preferred_element_type=f32)
    reduced = jnp.dot(g, up, preferred_element_type=f32)
    high = reduced.astype(bf16)
    low = (reduced - high.astype(f32)).astype(bf16)
    both = jnp.concatenate([high, low], axis=1)
    out_part = lax.dot_general(rank_twice, both, nt, preferred_element_type=f32)
    out_ref[i * sub : (i + 1) * sub, :] = in_part.astype(out_ref.dtype)
    for side in range(2):
        for piece in range(sub // lanes):
            row = tokens + side * stack + (i * (sub // lanes) + piece) * out_width
            out_ref[row : row + out_width, :] = out_part[
                side * out_width : (side + 1) * out_width, piece * lanes : (piece + 1) * lanes
            ].astype(out_ref.dtype)


def project_send_kernel(
    x_hbm, g_hbm, w_hbm, up_hbm, rank_hbm, out_ref, x_mine, g_mine, w, up, x, g, rank, sems
):
    core, _ = position()
    steps, sub = x.shape[:2]
    tokens = steps * sub

    def rows(half, i):
        return pl.ds(pl.multiple_of((half * steps + i) * sub, sub), sub)

    started = [
        pltpu.make_async_copy(w_hbm, w, sems.at[0]),
        pltpu.make_async_copy(up_hbm, up, sems.at[1]),
        pltpu.make_async_copy(rank_hbm, rank, sems.at[2]),
    ]
    for i in range(steps):
        part = rows(1 - core, i)
        started.append(pltpu.make_async_copy(x_hbm.at[part, :], x.at[i], sems.at[len(started)]))
        started.append(pltpu.make_async_copy(g_hbm.at[part, :], g.at[i], sems.at[len(started)]))
    part = pl.ds(pl.multiple_of(core * tokens, tokens), tokens)
    started.append(pltpu.make_async_copy(x_hbm.at[part, :], x_mine, sems.at[len(started)]))
    started.append(pltpu.make_async_copy(g_hbm.at[part, :], g_mine, sems.at[len(started)]))
    for copy in started:
        copy.start()
    for copy in started[:3]:
        copy.wait()
    rank_twice = jnp.concatenate([rank[...], rank[...]], axis=1)
    for i in range(steps):
        started[3 + 2 * i].wait()
        started[4 + 2 * i].wait()
        project_rows(x[i], g[i], w[...], up[...], rank_twice, out_ref, i, tokens)
    started[-2].wait()
    started[-1].wait()


def project_keep_kernel(x, g, w, up, rank, out_ref):
    rank_twice = jnp.concatenate([rank[...], rank[...]], axis=1)
    tokens = x.shape[0]
    sub = min(512, tokens)
    for i in range(tokens // sub):
        part = slice(i * sub, (i + 1) * sub)
        project_rows(x[part, :], g[part, :], w[...], up[...], rank_twice, out_ref, i, tokens)


def project_send(x, g, w, up, rank):
    tokens, depth = x.shape[0] // 2, x.shape[1]
    sub = min(512, tokens)
    steps = tokens // sub
    rows = tokens + tokens // lanes * rank.shape[0]
    vmem = pl.BlockSpec(memory_space=pltpu.VMEM)
    return pl.pallas_call(
        project_send_kernel,
        in_specs=[pl.BlockSpec(memory_space=pltpu.HBM)] * 5,
        out_specs=[vmem] * 5,
        out_shape=[
            jax.ShapeDtypeStruct((rows, lanes), bf16),
            pltpu.VMEM((tokens, depth), bf16),
            pltpu.VMEM((tokens, depth), bf16),
            pltpu.VMEM(w.shape, bf16),
            pltpu.VMEM(up.shape, bf16),
        ],
        scratch_shapes=[
            pltpu.VMEM((steps, sub, depth), bf16),
            pltpu.VMEM((steps, sub, depth), bf16),
            pltpu.VMEM(rank.shape, bf16),
            pltpu.SemaphoreType.DMA((2 * steps + 5,)),
        ],
        compiler_params=params(24),
        cost_estimate=cost(4 * tokens * depth * lanes, 8 * tokens * depth),
        name="project_send",
    )(*(pltpu.with_memory_space_constraint(array, pltpu.HBM) for array in (x, g, w, up, rank)))


def project_keep(x, g, w, up, rank):
    tokens, depth = x.shape
    rows = tokens + tokens // lanes * rank.shape[0]
    vmem = pl.BlockSpec(memory_space=pltpu.VMEM)
    return pl.pallas_call(
        project_keep_kernel,
        in_specs=[vmem] * 5,
        out_specs=vmem,
        out_shape=jax.ShapeDtypeStruct((rows, lanes), f32),
        compiler_params=params(16),
        cost_estimate=cost(4 * tokens * depth * lanes, 4 * tokens * depth),
        name="project_keep",
    )(*(pltpu.with_memory_space_constraint(array, pltpu.VMEM) for array in (x, g, w, up)), rank)


def square_kernel(targets_hbm, squares_ref, targets, sems):
    parts, rows, depth = targets.shape
    started = []
    for i in range(parts):
        part = pl.ds(i * rows, rows)
        started.append(pltpu.make_async_copy(targets_hbm.at[part, :], targets.at[i], sems.at[i]))
        started[-1].start()
    lane = lax.broadcasted_iota(jnp.int32, (lanes, lanes), 1)
    squares = jnp.zeros((lanes, lanes), f32)
    for i in range(parts):
        started[i].wait()
        for first in range(0, rows, lanes):
            totals = jnp.zeros((lanes, lanes), f32)
            for k in range(depth // lanes):
                wide = targets[i, first : first + lanes, k * lanes : (k + 1) * lanes].astype(f32)
                totals += wide * wide
            total = jnp.sum(totals, axis=1, keepdims=True)
            squares = jnp.where(lane == (i * rows + first) // lanes, total, squares)
    squares_ref[...] = squares


def column_squares(targets):
    columns, depth = targets.shape
    rows = min(256, columns)
    return pl.pallas_call(
        square_kernel,
        in_specs=[pl.BlockSpec(memory_space=pltpu.HBM)],
        out_specs=pl.BlockSpec(memory_space=pltpu.VMEM),
        out_shape=jax.ShapeDtypeStruct((lanes, lanes), f32),
        scratch_shapes=[
            pltpu.VMEM((columns // rows, rows, depth), targets.dtype),
            pltpu.SemaphoreType.DMA((columns // rows,)),
        ],
        compiler_params=params(16),
        cost_estimate=cost(2 * columns * depth, 2 * columns * depth),
        name="squares",
    )(pltpu.with_memory_space_constraint(targets, pltpu.HBM))


def stage_kernel(targets_hbm, targets_ref, sem):
    copy = pltpu.make_async_copy(targets_hbm, targets_ref, sem)
    copy.start()
    copy.wait()


def stage(targets):
    return pl.pallas_call(
        stage_kernel,
        in_specs=[pl.BlockSpec(memory_space=pltpu.HBM)],
        out_specs=pl.BlockSpec(memory_space=pltpu.VMEM),
        out_shape=pltpu.VMEM(targets.shape, targets.dtype),
        scratch_shapes=[pltpu.SemaphoreType.DMA],
        compiler_params=params(12),
        cost_estimate=cost(0, 2 * targets.size),
        name="stage",
    )(pltpu.with_memory_space_constraint(targets, pltpu.HBM))


def core_sum_kernel(parts, length, keep_ref, came_ref, *outs):
    sends, lefts = outs[:chunks], outs[chunks:]
    rows = keep_ref.shape[0]
    tokens = sum(number for _, number in parts) * length
    stack = (rows - tokens) // 2
    _, x = position()
    for (first, number), send_ref, left_ref in zip(parts, sends, lefts):
        size = number * length
        part = slice(first * length, first * length + size)
        total = keep_ref[part, :] + came_ref[part, :].astype(f32)
        send_ref[:size, :] = total.astype(bf16)
        left_ref[:size, :] = total
        height = stack * size // tokens
        for side, ref in ((1 - x, send_ref), (x, left_ref)):
            start = tokens + side * stack + stack * first * length // tokens
            part = pl.ds(pl.multiple_of(start, 32), height)
            total = keep_ref[part, :] + came_ref[part, :].astype(f32)
            ref[size:, :] = total.astype(ref.dtype)


def core_sum(keep, came, parts, length):
    rows = keep.shape[0]
    tokens = sum(number for _, number in parts) * length
    heights = [(tokens + (rows - tokens) // 2) * number * length // tokens for _, number in parts]
    vmem = pl.BlockSpec(memory_space=pltpu.VMEM)
    outs = pl.pallas_call(
        functools.partial(core_sum_kernel, parts, length),
        in_specs=[vmem, vmem],
        out_specs=[vmem] * (2 * chunks),
        out_shape=[jax.ShapeDtypeStruct((height, lanes), dtype) for dtype in (bf16, f32) for height in heights],
        compiler_params=params(8),
        cost_estimate=cost(rows * lanes, 12 * rows * lanes),
        name="core_sum",
    )(keep, came)
    return list(outs[:chunks]), list(outs[chunks:])


def feature_kernel(first, core_programs, programs, lengths, left_ref, came_ref, mine_ref, other_ref, held):
    core, _ = position()
    quarter = mine_ref.shape[0]
    out_width = 2 * quarter
    final = left_ref.shape[0]
    tokens = final * lanes // (lanes + out_width)
    length = tokens // programs
    some = 8
    span = some * length
    program = lax.broadcasted_iota(jnp.int32, (some, span), 0)
    token = lax.broadcasted_iota(jnp.int32, (some, span), 1) - program * length
    for group in range(programs // some):
        rows = slice(group * span, (group + 1) * span)
        in_sum = (left_ref[rows, :] + came_ref[rows, :].astype(f32)).astype(bf16)
        start = tokens + group * (span // lanes) * out_width
        rows = slice(start, start + span // lanes * out_width)
        out_sum = left_ref[rows, :] + came_ref[rows, :].astype(f32)
        out_rows = jnp.concatenate(
            [out_sum[i * out_width : (i + 1) * out_width, :] for i in range(span // lanes)], axis=1
        )
        limit = jnp.zeros((some, span), jnp.int32)
        for s in range(some):
            limit = jnp.where(program == s, lengths[core * core_programs + first + group * some + s], limit)
        live = ((token >= 0) & (token < limit)).astype(f32)
        spread = (out_rows[:, None, :] * live[None, :, :]).reshape(out_width * some, span)
        made = jnp.dot(spread.astype(bf16), in_sum, preferred_element_type=f32)
        held[:, group * some : (group + 1) * some, :] = made.reshape(out_width, some, lanes)
    mine_ref[...] = held[pl.ds(core * quarter, quarter), :, :].astype(bf16)
    other_ref[...] = held[pl.ds((1 - core) * quarter, quarter), :, :].astype(bf16)


def make_features(first, core_programs, programs, quarter, lengths, left, came):
    vmem = pl.BlockSpec(memory_space=pltpu.VMEM)
    shape = jax.ShapeDtypeStruct((quarter, programs, lanes), bf16)
    return pl.pallas_call(
        functools.partial(feature_kernel, first, core_programs, programs),
        in_specs=[pl.BlockSpec(memory_space=pltpu.SMEM), vmem, vmem],
        out_specs=[vmem, vmem],
        out_shape=[shape, shape],
        scratch_shapes=[pltpu.VMEM((2 * quarter, programs, lanes), f32)],
        compiler_params=params(12),
        cost_estimate=cost(10**8, 8 * left.size),
        name="features",
    )(lengths, left, came)


def score_kernel(count, far, order_ref, squares_ref, targets_ref, *refs):
    pieces, sends, (keep_ref, ordered) = refs[:count], refs[count:-2], refs[-2:]
    columns, rows = targets_ref.shape[0], keep_ref.shape[0]

    def store(first, size, values):
        height = rows // len(sends)
        for i, ref in enumerate(sends):
            ref[:, first : first + size] = values[i * height : (i + 1) * height, :]
        keep_ref[:, first : first + size] = values[rows:, :]

    core, x = position()
    x = 1 - x if far else x
    position_rows = order_ref[...]
    row = lax.broadcasted_iota(jnp.int32, (2 * rows, position_rows.shape[1]), 0)
    first = jnp.where(row < rows, (x * 2 + 1 - core) * rows, (x * 2 + core) * rows - rows)
    chosen = (row + first == position_rows).astype(bf16)
    totals = jnp.zeros((2 * rows, lanes), f32)
    halves = pieces
    while any(ref.ndim > 3 for ref in halves):
        halves = [half for ref in halves for half in ([ref.at[i] for i in range(ref.shape[0])] if ref.ndim > 3 else [ref])]
    for a in range(0, halves[0].shape[0], 2):
        block = jnp.concatenate(
            [
                jnp.concatenate([half[a + d] for half in halves], axis=0)
                for d in range(2)
            ],
            axis=1,
        )
        found = jnp.dot(chosen, block, preferred_element_type=f32)
        ordered[:, a * lanes : (a + 2) * lanes] = found.astype(bf16)
        totals += found[:, :lanes] * found[:, :lanes] + found[:, lanes:] * found[:, lanes:]
    lane = lax.broadcasted_iota(jnp.int32, (2 * rows, lanes), 1)
    row_squares = jnp.sum(totals, axis=1, keepdims=True)
    spare = jnp.zeros((rows - lanes, lanes), f32)
    squares = jnp.concatenate([squares_ref[...], spare] * 2 if rows > lanes else [squares_ref[...]] * 2, axis=0)
    store(columns, lanes, jnp.where(lane == middle, row_squares, squares).astype(bf16))
    tile = min(512, columns)
    for j in range(0, columns, tile):
        scores = lax.dot_general(
            ordered[...], targets_ref[j : j + tile, :], nt, preferred_element_type=f32
        ).astype(bf16)
        store(j, tile, scores)


def partial_scores(far, order, squares, pieces, targets, rows):
    columns, depth = targets.shape
    held = 2 * (4 * rows * depth + 4 * rows * columns + 8 * rows * order.size)
    limit = 6 + held // 1024**2
    vmem = pl.BlockSpec(memory_space=pltpu.VMEM)
    sends = 1 if far else 2
    shape = jax.ShapeDtypeStruct((rows // sends, columns + lanes), bf16)
    whole = jax.ShapeDtypeStruct((rows, columns + lanes), bf16)
    return pl.pallas_call(
        functools.partial(score_kernel, len(pieces), far),
        in_specs=[vmem] * (3 + len(pieces)),
        out_specs=[vmem] * (sends + 1),
        out_shape=[shape] * sends + [whole],
        scratch_shapes=[pltpu.VMEM((2 * rows, depth), bf16)],
        compiler_params=params(limit),
        cost_estimate=cost(4 * rows * columns * depth, 2 * columns * depth),
        name="scores_far" if far else "scores_near",
    )(order, squares, pltpu.with_memory_space_constraint(targets, pltpu.VMEM), *pieces)


def join_kernel(keep_ref, came_ref, out_ref):
    out_ref[...] = (keep_ref[...].astype(f32) + came_ref[...].astype(f32)).astype(bf16)


def join(keep, came):
    vmem = pl.BlockSpec(memory_space=pltpu.VMEM)
    return pl.pallas_call(
        join_kernel,
        in_specs=[vmem, vmem],
        out_specs=vmem,
        out_shape=jax.ShapeDtypeStruct(keep.shape, bf16),
        compiler_params=params(16),
        cost_estimate=cost(keep.size, 6 * keep.size),
        name="join",
    )(keep, came)


def finish_kernel(root_count, keep_ref, low_ref, high_ref, far_ref, out_ref):
    columns = out_ref.shape[1]
    height = low_ref.shape[0]

    def total(i, first, size):
        rows, strip = slice(i * height, (i + 1) * height), slice(first, first + size)
        mine = keep_ref[rows, strip].astype(f32) + (low_ref, high_ref)[i][:, strip].astype(f32)
        return mine + far_ref[rows, strip].astype(f32)

    squares = jnp.concatenate([total(i, columns, lanes) for i in range(2)], axis=0)
    row_scale = lax.rsqrt(squares[:, middle : middle + 1] + epsilon) * root_count
    column_scale = lax.rsqrt(squares[:lanes, :].T + epsilon)
    for i in range(2):
        rows = slice(i * height, (i + 1) * height)
        for q in range(columns // lanes):
            scaled = total(i, q * lanes, lanes) * row_scale[rows, :] * column_scale[q : q + 1, :]
            out_ref[rows, q * lanes : (q + 1) * lanes] = scaled


def finish(root_count, keep, low, high, far):
    rows, columns = keep.shape[0], keep.shape[1] - lanes
    vmem = pl.BlockSpec(memory_space=pltpu.VMEM)
    return pl.pallas_call(
        functools.partial(finish_kernel, root_count),
        in_specs=[vmem] * 4,
        out_specs=vmem,
        out_shape=jax.ShapeDtypeStruct((rows, columns), f32),
        compiler_params=params(24),
        cost_estimate=cost(4 * rows * columns, 10 * rows * columns),
        name="finish",
    )(keep, low, high, far)


def shards(
    layer_input_rows,
    output_gradient_rows,
    adapter_up_weight,
    input_side_projection,
    rank_side_projection,
    lengths,
    program_output_index,
    targets,
):
    wide_count, narrow_count = lax.axis_size("wide"), lax.axis_size("narrow")
    w, n = lax.axis_index("wide"), lax.axis_index("narrow")
    core, x = n % 2, n // 2
    programs = lengths.shape[0]
    length = layer_input_rows.shape[0] // programs
    quarter = rank_side_projection.shape[1] // narrow_count
    share = programs // 2
    parts = parts_of(share)
    rank = rank_side_projection.T
    send, *staged = project_send(
        layer_input_rows, output_gradient_rows, input_side_projection, adapter_up_weight, rank
    )
    keep = project_keep(*staged, rank)
    sends, lefts = core_sum(keep, exchange(send, "narrow", 1), parts, length)
    squares = column_squares(after(targets, sends[0]))
    lefts[0], squares = lax.optimization_barrier((lefts[0], squares))
    blocks = []
    for i in range(chunks):
        came = exchange(sends[i], "narrow", 2)
        left = after(lefts[i], *blocks) if blocks else lefts[i]
        mine, other = make_features(parts[i][0], share, parts[i][1], quarter, lengths, left, came)
        blocks.append(jnp.stack([mine, exchange(other, "narrow", 1)]))
    pieces = gather_blocks(blocks)
    targets = stage(after(targets, pieces[-2][-1]))
    pieces = [chunk for piece in pieces for chunk in piece]

    order = program_output_index.reshape(wide_count, 2, share)
    order = jnp.take(order, w ^ jnp.arange(wide_count), axis=0)
    order = jnp.where(core == 1, order[:, ::-1], order)
    order = [order[:, :, first : first + number].reshape(wide_count, -1) for first, number in parts]
    order = jnp.concatenate(order, axis=1).reshape(1, -1)
    rows = order.shape[1] // narrow_count

    far_send, far_keep = partial_scores(True, order, squares, pieces, targets, rows)
    far = join(far_keep, exchange(far_send, "narrow", 1))
    order, far = lax.optimization_barrier((order, far))
    far = exchange(far, "narrow", 2)
    *near_sends, near_keep = partial_scores(False, order, squares, pieces, targets, rows)
    near = [exchange(part, "narrow", 1) for part in near_sends]
    root_count = math.sqrt(float(targets.shape[1] * narrow_count))
    return finish(root_count, near_keep, *near, far)


def solution(mesh):
    return jax.shard_map(
        shards,
        mesh=mesh,
        in_specs=(
            P("wide", "narrow"),
            P("wide", "narrow"),
            P("narrow", None),
            P("narrow", None),
            P(),
            P("wide"),
            P(),
            P("wide", "narrow"),
        ),
        out_specs=P("narrow", "wide"),
        check_vma=False,
    )
```

```python
import functools
import math

import jax
import jax.numpy as jnp
from jax import lax
from jax.experimental import pallas as pl
from jax.experimental.pallas import tpu as pltpu
from jax.sharding import PartitionSpec as P

epsilon = 1e-06
lanes = 128
chunks = 2
middle = lanes // 2
f32, bf16 = jnp.float32, jnp.bfloat16
nt = (((1,), (1,)), ((), ()))


def params(mebibytes):
    return pltpu.CompilerParams(vmem_limit_bytes=int(mebibytes * 1024 * 1024))


def cost(flops, moved):
    return pl.CostEstimate(flops=flops, bytes_accessed=moved, transcendentals=0)


def exchange(array, axis, bit):
    count = lax.axis_size(axis)
    return lax.ppermute(array, axis, [(i, i ^ bit) for i in range(count)])


def after(array, *others):
    return lax.optimization_barrier((array,) + others)[0]


def gather_blocks(blocks):
    count = lax.axis_size("wide")
    if count == 8 and chunks == 2:
        first, second = blocks
        far = [exchange(first, "wide", 4)]
        above = [exchange(first, "wide", 2)]
        beside = [exchange(first, "wide", 1)]
        second = after(second, far[0])
        far.append(exchange(second, "wide", 4))
        across = [exchange(far[0], "wide", 2)]
        far_beside = [exchange(after(far[0], beside[0], above[0]), "wide", 1)]
        beside.append(exchange(second, "wide", 1))
        above.append(exchange(second, "wide", 2))
        across.append(exchange(far[1], "wide", 2))
        far_beside.append(exchange(after(far[1], beside[1], above[1]), "wide", 1))
        across_beside = [exchange(chunk, "wide", 1) for chunk in across]
        above_beside = [
            exchange(after(chunk, there), "wide", 2) for chunk, there in zip(beside, (far[1], across[0]))
        ]
        return blocks, beside, above, above_beside, far, far_beside, across, across_beside
    held = {0: blocks}
    bit = count // 2
    while bit:
        for k in list(held):
            held[k | bit] = [exchange(chunk, "wide", bit) for chunk in held[k]]
        bit //= 2
    return [held[k] for k in range(count)]


def parts_of(programs):
    number = programs // chunks
    return [(i * number, number) for i in range(chunks)]


def position():
    n = lax.axis_index("narrow")
    return n % 2, n // 2


def project_rows(x, g, w, up, rank_twice, out_ref, i, tokens):
    sub = x.shape[0]
    out_width = rank_twice.shape[0] // 2
    stack = tokens // lanes * out_width
    in_part = jnp.dot(x, w, preferred_element_type=f32)
    reduced = jnp.dot(g, up, preferred_element_type=f32)
    high = reduced.astype(bf16)
    low = (reduced - high.astype(f32)).astype(bf16)
    both = jnp.concatenate([high, low], axis=1)
    out_part = lax.dot_general(rank_twice, both, nt, preferred_element_type=f32)
    out_ref[i * sub : (i + 1) * sub, :] = in_part.astype(out_ref.dtype)
    for side in range(2):
        for piece in range(sub // lanes):
            row = tokens + side * stack + (i * (sub // lanes) + piece) * out_width
            out_ref[row : row + out_width, :] = out_part[
                side * out_width : (side + 1) * out_width, piece * lanes : (piece + 1) * lanes
            ].astype(out_ref.dtype)


def project_send_kernel(
    x_hbm, g_hbm, w_hbm, up_hbm, rank_hbm, out_ref, x_mine, g_mine, w, up, x, g, rank, sems
):
    core, _ = position()
    steps, sub = x.shape[:2]
    tokens = steps * sub

    def rows(half, i):
        return pl.ds(pl.multiple_of((half * steps + i) * sub, sub), sub)

    started = [
        pltpu.make_async_copy(w_hbm, w, sems.at[0]),
        pltpu.make_async_copy(up_hbm, up, sems.at[1]),
        pltpu.make_async_copy(rank_hbm, rank, sems.at[2]),
    ]
    for i in range(steps):
        part = rows(1 - core, i)
        started.append(pltpu.make_async_copy(x_hbm.at[part, :], x.at[i], sems.at[len(started)]))
        started.append(pltpu.make_async_copy(g_hbm.at[part, :], g.at[i], sems.at[len(started)]))
    part = pl.ds(pl.multiple_of(core * tokens, tokens), tokens)
    started.append(pltpu.make_async_copy(x_hbm.at[part, :], x_mine, sems.at[len(started)]))
    started.append(pltpu.make_async_copy(g_hbm.at[part, :], g_mine, sems.at[len(started)]))
    for copy in started:
        copy.start()
    for copy in started[:3]:
        copy.wait()
    rank_twice = jnp.concatenate([rank[...], rank[...]], axis=1)
    for i in range(steps):
        started[3 + 2 * i].wait()
        started[4 + 2 * i].wait()
        project_rows(x[i], g[i], w[...], up[...], rank_twice, out_ref, i, tokens)
    started[-2].wait()
    started[-1].wait()


def project_keep_kernel(x, g, w, up, rank, out_ref):
    rank_twice = jnp.concatenate([rank[...], rank[...]], axis=1)
    tokens = x.shape[0]
    sub = min(512, tokens)
    for i in range(tokens // sub):
        part = slice(i * sub, (i + 1) * sub)
        project_rows(x[part, :], g[part, :], w[...], up[...], rank_twice, out_ref, i, tokens)


def project_send(x, g, w, up, rank):
    tokens, depth = x.shape[0] // 2, x.shape[1]
    sub = min(512, tokens)
    steps = tokens // sub
    rows = tokens + tokens // lanes * rank.shape[0]
    vmem = pl.BlockSpec(memory_space=pltpu.VMEM)
    return pl.pallas_call(
        project_send_kernel,
        in_specs=[pl.BlockSpec(memory_space=pltpu.HBM)] * 5,
        out_specs=[vmem] * 5,
        out_shape=[
            jax.ShapeDtypeStruct((rows, lanes), bf16),
            pltpu.VMEM((tokens, depth), bf16),
            pltpu.VMEM((tokens, depth), bf16),
            pltpu.VMEM(w.shape, bf16),
            pltpu.VMEM(up.shape, bf16),
        ],
        scratch_shapes=[
            pltpu.VMEM((steps, sub, depth), bf16),
            pltpu.VMEM((steps, sub, depth), bf16),
            pltpu.VMEM(rank.shape, bf16),
            pltpu.SemaphoreType.DMA((2 * steps + 5,)),
        ],
        compiler_params=params(24),
        cost_estimate=cost(4 * tokens * depth * lanes, 8 * tokens * depth),
        name="project_send",
    )(*(pltpu.with_memory_space_constraint(array, pltpu.HBM) for array in (x, g, w, up, rank)))


def project_keep(x, g, w, up, rank):
    tokens, depth = x.shape
    rows = tokens + tokens // lanes * rank.shape[0]
    vmem = pl.BlockSpec(memory_space=pltpu.VMEM)
    return pl.pallas_call(
        project_keep_kernel,
        in_specs=[vmem] * 5,
        out_specs=vmem,
        out_shape=jax.ShapeDtypeStruct((rows, lanes), f32),
        compiler_params=params(16),
        cost_estimate=cost(4 * tokens * depth * lanes, 4 * tokens * depth),
        name="project_keep",
    )(*(pltpu.with_memory_space_constraint(array, pltpu.VMEM) for array in (x, g, w, up)), rank)


def square_kernel(targets_hbm, squares_ref, targets, sems):
    parts, rows, depth = targets.shape
    started = []
    for i in range(parts):
        part = pl.ds(i * rows, rows)
        started.append(pltpu.make_async_copy(targets_hbm.at[part, :], targets.at[i], sems.at[i]))
        started[-1].start()
    lane = lax.broadcasted_iota(jnp.int32, (lanes, lanes), 1)
    squares = jnp.zeros((lanes, lanes), f32)
    for i in range(parts):
        started[i].wait()
        for first in range(0, rows, lanes):
            totals = jnp.zeros((lanes, lanes), f32)
            for k in range(depth // lanes):
                wide = targets[i, first : first + lanes, k * lanes : (k + 1) * lanes].astype(f32)
                totals += wide * wide
            total = jnp.sum(totals, axis=1, keepdims=True)
            squares = jnp.where(lane == (i * rows + first) // lanes, total, squares)
    squares_ref[...] = squares


def column_squares(targets):
    columns, depth = targets.shape
    rows = min(256, columns)
    return pl.pallas_call(
        square_kernel,
        in_specs=[pl.BlockSpec(memory_space=pltpu.HBM)],
        out_specs=pl.BlockSpec(memory_space=pltpu.VMEM),
        out_shape=jax.ShapeDtypeStruct((lanes, lanes), f32),
        scratch_shapes=[
            pltpu.VMEM((columns // rows, rows, depth), targets.dtype),
            pltpu.SemaphoreType.DMA((columns // rows,)),
        ],
        compiler_params=params(16),
        cost_estimate=cost(2 * columns * depth, 2 * columns * depth),
        name="squares",
    )(pltpu.with_memory_space_constraint(targets, pltpu.HBM))


def stage_kernel(targets_hbm, targets_ref, sem):
    copy = pltpu.make_async_copy(targets_hbm, targets_ref, sem)
    copy.start()
    copy.wait()


def stage(targets):
    return pl.pallas_call(
        stage_kernel,
        in_specs=[pl.BlockSpec(memory_space=pltpu.HBM)],
        out_specs=pl.BlockSpec(memory_space=pltpu.VMEM),
        out_shape=pltpu.VMEM(targets.shape, targets.dtype),
        scratch_shapes=[pltpu.SemaphoreType.DMA],
        compiler_params=params(12),
        cost_estimate=cost(0, 2 * targets.size),
        name="stage",
    )(pltpu.with_memory_space_constraint(targets, pltpu.HBM))


def core_sum_kernel(parts, length, keep_ref, came_ref, *outs):
    sends, lefts = outs[:chunks], outs[chunks:]
    rows = keep_ref.shape[0]
    tokens = sum(number for _, number in parts) * length
    stack = (rows - tokens) // 2
    _, x = position()
    for (first, number), send_ref, left_ref in zip(parts, sends, lefts):
        size = number * length
        part = slice(first * length, first * length + size)
        total = keep_ref[part, :] + came_ref[part, :].astype(f32)
        send_ref[:size, :] = total.astype(bf16)
        left_ref[:size, :] = total
        height = stack * size // tokens
        for side, ref in ((1 - x, send_ref), (x, left_ref)):
            start = tokens + side * stack + stack * first * length // tokens
            part = pl.ds(pl.multiple_of(start, 32), height)
            total = keep_ref[part, :] + came_ref[part, :].astype(f32)
            ref[size:, :] = total.astype(ref.dtype)


def core_sum(keep, came, parts, length):
    rows = keep.shape[0]
    tokens = sum(number for _, number in parts) * length
    heights = [(tokens + (rows - tokens) // 2) * number * length // tokens for _, number in parts]
    vmem = pl.BlockSpec(memory_space=pltpu.VMEM)
    outs = pl.pallas_call(
        functools.partial(core_sum_kernel, parts, length),
        in_specs=[vmem, vmem],
        out_specs=[vmem] * (2 * chunks),
        out_shape=[jax.ShapeDtypeStruct((height, lanes), dtype) for dtype in (bf16, f32) for height in heights],
        compiler_params=params(8),
        cost_estimate=cost(rows * lanes, 12 * rows * lanes),
        name="core_sum",
    )(keep, came)
    return list(outs[:chunks]), list(outs[chunks:])


def feature_kernel(first, core_programs, programs, lengths, left_ref, came_ref, mine_ref, other_ref, held):
    core, _ = position()
    quarter = mine_ref.shape[0]
    out_width = 2 * quarter
    final = left_ref.shape[0]
    tokens = final * lanes // (lanes + out_width)
    length = tokens // programs
    some = 8
    span = some * length
    program = lax.broadcasted_iota(jnp.int32, (some, span), 0)
    token = lax.broadcasted_iota(jnp.int32, (some, span), 1) - program * length
    for group in range(programs // some):
        rows = slice(group * span, (group + 1) * span)
        in_sum = (left_ref[rows, :] + came_ref[rows, :].astype(f32)).astype(bf16)
        start = tokens + group * (span // lanes) * out_width
        rows = slice(start, start + span // lanes * out_width)
        out_sum = left_ref[rows, :] + came_ref[rows, :].astype(f32)
        out_rows = jnp.concatenate(
            [out_sum[i * out_width : (i + 1) * out_width, :] for i in range(span // lanes)], axis=1
        )
        limit = jnp.zeros((some, span), jnp.int32)
        for s in range(some):
            limit = jnp.where(program == s, lengths[core * core_programs + first + group * some + s], limit)
        live = ((token >= 0) & (token < limit)).astype(f32)
        spread = (out_rows[:, None, :] * live[None, :, :]).reshape(out_width * some, span)
        made = jnp.dot(spread.astype(bf16), in_sum, preferred_element_type=f32)
        held[:, group * some : (group + 1) * some, :] = made.reshape(out_width, some, lanes)
    mine_ref[...] = held[pl.ds(core * quarter, quarter), :, :].astype(bf16)
    other_ref[...] = held[pl.ds((1 - core) * quarter, quarter), :, :].astype(bf16)


def make_features(first, core_programs, programs, quarter, lengths, left, came):
    vmem = pl.BlockSpec(memory_space=pltpu.VMEM)
    shape = jax.ShapeDtypeStruct((quarter, programs, lanes), bf16)
    return pl.pallas_call(
        functools.partial(feature_kernel, first, core_programs, programs),
        in_specs=[pl.BlockSpec(memory_space=pltpu.SMEM), vmem, vmem],
        out_specs=[vmem, vmem],
        out_shape=[shape, shape],
        scratch_shapes=[pltpu.VMEM((2 * quarter, programs, lanes), f32)],
        compiler_params=params(12),
        cost_estimate=cost(10**8, 8 * left.size),
        name="features",
    )(lengths, left, came)


def score_kernel(count, far, order_ref, squares_ref, targets_ref, *refs):
    pieces, sends, (keep_ref, ordered) = refs[:count], refs[count:-2], refs[-2:]
    columns, rows = targets_ref.shape[0], keep_ref.shape[0]

    def store(first, size, values):
        height = rows // len(sends)
        for i, ref in enumerate(sends):
            ref[:, first : first + size] = values[i * height : (i + 1) * height, :]
        keep_ref[:, first : first + size] = values[rows:, :]

    core, x = position()
    x = 1 - x if far else x
    position_rows = order_ref[...]
    row = lax.broadcasted_iota(jnp.int32, (2 * rows, position_rows.shape[1]), 0)
    first = jnp.where(row < rows, (x * 2 + 1 - core) * rows, (x * 2 + core) * rows - rows)
    chosen = (row + first == position_rows).astype(bf16)
    totals = jnp.zeros((2 * rows, lanes), f32)
    halves = pieces
    while any(ref.ndim > 3 for ref in halves):
        halves = [half for ref in halves for half in ([ref.at[i] for i in range(ref.shape[0])] if ref.ndim > 3 else [ref])]
    for a in range(0, halves[0].shape[0], 2):
        block = jnp.concatenate(
            [
                jnp.concatenate([half[a + d] for half in halves], axis=0)
                for d in range(2)
            ],
            axis=1,
        )
        found = jnp.dot(chosen, block, preferred_element_type=f32)
        ordered[:, a * lanes : (a + 2) * lanes] = found.astype(bf16)
        totals += found[:, :lanes] * found[:, :lanes] + found[:, lanes:] * found[:, lanes:]
    lane = lax.broadcasted_iota(jnp.int32, (2 * rows, lanes), 1)
    row_squares = jnp.sum(totals, axis=1, keepdims=True)
    spare = jnp.zeros((rows - lanes, lanes), f32)
    squares = jnp.concatenate([squares_ref[...], spare] * 2 if rows > lanes else [squares_ref[...]] * 2, axis=0)
    store(columns, lanes, jnp.where(lane == middle, row_squares, squares).astype(bf16))
    tile = min(512, columns)
    for j in range(0, columns, tile):
        scores = lax.dot_general(
            ordered[...], targets_ref[j : j + tile, :], nt, preferred_element_type=f32
        ).astype(bf16)
        store(j, tile, scores)


def partial_scores(far, order, squares, pieces, targets, rows):
    columns, depth = targets.shape
    held = 2 * (4 * rows * depth + 4 * rows * columns + 8 * rows * order.size)
    limit = 6 + held // 1024**2
    vmem = pl.BlockSpec(memory_space=pltpu.VMEM)
    sends = 1 if far else 2
    shape = jax.ShapeDtypeStruct((rows // sends, columns + lanes), bf16)
    whole = jax.ShapeDtypeStruct((rows, columns + lanes), bf16)
    return pl.pallas_call(
        functools.partial(score_kernel, len(pieces), far),
        in_specs=[vmem] * (3 + len(pieces)),
        out_specs=[vmem] * (sends + 1),
        out_shape=[shape] * sends + [whole],
        scratch_shapes=[pltpu.VMEM((2 * rows, depth), bf16)],
        compiler_params=params(limit),
        cost_estimate=cost(4 * rows * columns * depth, 2 * columns * depth),
        name="scores_far" if far else "scores_near",
    )(order, squares, pltpu.with_memory_space_constraint(targets, pltpu.VMEM), *pieces)


def join_kernel(keep_ref, came_ref, out_ref):
    out_ref[...] = (keep_ref[...].astype(f32) + came_ref[...].astype(f32)).astype(bf16)


def join(keep, came):
    vmem = pl.BlockSpec(memory_space=pltpu.VMEM)
    return pl.pallas_call(
        join_kernel,
        in_specs=[vmem, vmem],
        out_specs=vmem,
        out_shape=jax.ShapeDtypeStruct(keep.shape, bf16),
        compiler_params=params(16),
        cost_estimate=cost(keep.size, 6 * keep.size),
        name="join",
    )(keep, came)


def finish_kernel(root_count, keep_ref, low_ref, high_ref, far_ref, out_ref):
    columns = out_ref.shape[1]
    height = low_ref.shape[0]

    def total(i, first, size):
        rows, strip = slice(i * height, (i + 1) * height), slice(first, first + size)
        mine = keep_ref[rows, strip].astype(f32) + (low_ref, high_ref)[i][:, strip].astype(f32)
        return mine + far_ref[rows, strip].astype(f32)

    squares = jnp.concatenate([total(i, columns, lanes) for i in range(2)], axis=0)
    row_scale = lax.rsqrt(squares[:, middle : middle + 1] + epsilon) * root_count
    column_scale = lax.rsqrt(squares[:lanes, :].T + epsilon)
    for i in range(2):
        rows = slice(i * height, (i + 1) * height)
        for q in range(columns // lanes):
            scaled = total(i, q * lanes, lanes) * row_scale[rows, :] * column_scale[q : q + 1, :]
            out_ref[rows, q * lanes : (q + 1) * lanes] = scaled


def finish(root_count, keep, low, high, far):
    rows, columns = keep.shape[0], keep.shape[1] - lanes
    vmem = pl.BlockSpec(memory_space=pltpu.VMEM)
    return pl.pallas_call(
        functools.partial(finish_kernel, root_count),
        in_specs=[vmem] * 4,
        out_specs=vmem,
        out_shape=jax.ShapeDtypeStruct((rows, columns), f32),
        compiler_params=params(24),
        cost_estimate=cost(4 * rows * columns, 10 * rows * columns),
        name="finish",
    )(keep, low, high, far)


def shards(
    layer_input_rows,
    output_gradient_rows,
    adapter_up_weight,
    input_side_projection,
    rank_side_projection,
    lengths,
    program_output_index,
    targets,
):
    wide_count, narrow_count = lax.axis_size("wide"), lax.axis_size("narrow")
    w, n = lax.axis_index("wide"), lax.axis_index("narrow")
    core, x = n % 2, n // 2
    programs = lengths.shape[0]
    length = layer_input_rows.shape[0] // programs
    quarter = rank_side_projection.shape[1] // narrow_count
    share = programs // 2
    parts = parts_of(share)
    rank = rank_side_projection.T
    send, *staged = project_send(
        layer_input_rows, output_gradient_rows, input_side_projection, adapter_up_weight, rank
    )
    keep = project_keep(*staged, rank)
    sends, lefts = core_sum(keep, exchange(send, "narrow", 1), parts, length)
    squares = column_squares(after(targets, sends[0]))
    lefts[0], squares = lax.optimization_barrier((lefts[0], squares))
    blocks = []
    for i in range(chunks):
        came = exchange(sends[i], "narrow", 2)
        left = after(lefts[i], *blocks) if blocks else lefts[i]
        mine, other = make_features(parts[i][0], share, parts[i][1], quarter, lengths, left, came)
        blocks.append(jnp.stack([mine, exchange(other, "narrow", 1)]))
    pieces = gather_blocks(blocks)
    targets = stage(after(targets, pieces[-2][-1]))
    pieces = [chunk for piece in pieces for chunk in piece]

    order = program_output_index.reshape(wide_count, 2, share)
    order = jnp.take(order, w ^ jnp.arange(wide_count), axis=0)
    order = jnp.where(core == 1, order[:, ::-1], order)
    order = [order[:, :, first : first + number].reshape(wide_count, -1) for first, number in parts]
    order = jnp.concatenate(order, axis=1).reshape(1, -1)
    rows = order.shape[1] // narrow_count

    far_send, far_keep = partial_scores(True, order, squares, pieces, targets, rows)
    far = join(far_keep, exchange(far_send, "narrow", 1))
    order, far = lax.optimization_barrier((order, far))
    far = exchange(far, "narrow", 2)
    *near_sends, near_keep = partial_scores(False, order, squares, pieces, targets, rows)
    near = [exchange(part, "narrow", 1) for part in near_sends]
    root_count = math.sqrt(float(targets.shape[1] * narrow_count))
    return finish(root_count, near_keep, *near, far)


def solution(mesh):
    return jax.shard_map(
        shards,
        mesh=mesh,
        in_specs=(
            P("wide", "narrow"),
            P("wide", "narrow"),
            P("narrow", None),
            P("narrow", None),
            P(),
            P("wide"),
            P(),
            P("wide", "narrow"),
        ),
        out_specs=P("narrow", "wide"),
        check_vma=False,
    )
```

```python
import functools
import math

import jax
import jax.numpy as jnp
from jax import lax
from jax.experimental import pallas as pl
from jax.experimental.pallas import tpu as pltpu
from jax.sharding import PartitionSpec as P

epsilon = 1e-06
lanes = 128
chunks = 2
middle = lanes // 2
f32, bf16 = jnp.float32, jnp.bfloat16
nt = (((1,), (1,)), ((), ()))


def params(mebibytes):
    return pltpu.CompilerParams(vmem_limit_bytes=int(mebibytes * 1024 * 1024))


def cost(flops, moved):
    return pl.CostEstimate(flops=flops, bytes_accessed=moved, transcendentals=0)


def exchange(array, axis, bit):
    count = lax.axis_size(axis)
    return lax.ppermute(array, axis, [(i, i ^ bit) for i in range(count)])


def after(array, *others):
    return lax.optimization_barrier((array,) + others)[0]


def gather_blocks(blocks):
    count = lax.axis_size("wide")
    if count == 8 and chunks == 2:
        first, second = blocks
        far = [exchange(first, "wide", 4)]
        above = [exchange(first, "wide", 2)]
        beside = [exchange(first, "wide", 1)]
        waiting, second = second, after(second, far[0])
        far.append(exchange(second, "wide", 4))
        across = [exchange(far[0], "wide", 2)]
        far_beside = [exchange(after(far[0], beside[0], above[0]), "wide", 1)]
        beside.append(exchange(after(waiting, beside[0]), "wide", 1))
        above.append(exchange(second, "wide", 2))
        across.append(exchange(far[1], "wide", 2))
        far_beside.append(exchange(after(far[1], beside[1], above[1]), "wide", 1))
        across_beside = [exchange(chunk, "wide", 1) for chunk in across]
        above_beside = [
            exchange(after(chunk, there), "wide", 2) for chunk, there in zip(beside, (far[1], across[0]))
        ]
        return blocks, beside, above, above_beside, far, far_beside, across, across_beside
    held = {0: blocks}
    bit = count // 2
    while bit:
        for k in list(held):
            held[k | bit] = [exchange(chunk, "wide", bit) for chunk in held[k]]
        bit //= 2
    return [held[k] for k in range(count)]


def parts_of(programs):
    number = programs // chunks
    return [(i * number, number) for i in range(chunks)]


def position():
    n = lax.axis_index("narrow")
    return n % 2, n // 2


def project_rows(x, g, w, up, rank_twice, out_ref, i, tokens):
    sub = x.shape[0]
    out_width = rank_twice.shape[0] // 2
    stack = tokens // lanes * out_width
    in_part = jnp.dot(x, w, preferred_element_type=f32)
    reduced = jnp.dot(g, up, preferred_element_type=f32)
    high = reduced.astype(bf16)
    low = (reduced - high.astype(f32)).astype(bf16)
    both = jnp.concatenate([high, low], axis=1)
    out_part = lax.dot_general(rank_twice, both, nt, preferred_element_type=f32)
    out_ref[i * sub : (i + 1) * sub, :] = in_part.astype(out_ref.dtype)
    for side in range(2):
        for piece in range(sub // lanes):
            row = tokens + side * stack + (i * (sub // lanes) + piece) * out_width
            out_ref[row : row + out_width, :] = out_part[
                side * out_width : (side + 1) * out_width, piece * lanes : (piece + 1) * lanes
            ].astype(out_ref.dtype)


def project_send_kernel(
    x_hbm, g_hbm, w_hbm, up_hbm, rank_hbm, out_ref, x_mine, g_mine, w, up, x, g, rank, sems
):
    core, _ = position()
    steps, sub = x.shape[:2]
    tokens = steps * sub

    def rows(half, i):
        return pl.ds(pl.multiple_of((half * steps + i) * sub, sub), sub)

    started = [
        pltpu.make_async_copy(w_hbm, w, sems.at[0]),
        pltpu.make_async_copy(up_hbm, up, sems.at[1]),
        pltpu.make_async_copy(rank_hbm, rank, sems.at[2]),
    ]
    for i in range(steps):
        part = rows(1 - core, i)
        started.append(pltpu.make_async_copy(x_hbm.at[part, :], x.at[i], sems.at[len(started)]))
        started.append(pltpu.make_async_copy(g_hbm.at[part, :], g.at[i], sems.at[len(started)]))
    part = pl.ds(pl.multiple_of(core * tokens, tokens), tokens)
    started.append(pltpu.make_async_copy(x_hbm.at[part, :], x_mine, sems.at[len(started)]))
    started.append(pltpu.make_async_copy(g_hbm.at[part, :], g_mine, sems.at[len(started)]))
    for copy in started:
        copy.start()
    for copy in started[:3]:
        copy.wait()
    rank_twice = jnp.concatenate([rank[...], rank[...]], axis=1)
    for i in range(steps):
        started[3 + 2 * i].wait()
        started[4 + 2 * i].wait()
        project_rows(x[i], g[i], w[...], up[...], rank_twice, out_ref, i, tokens)
    started[-2].wait()
    started[-1].wait()


def project_keep_kernel(x, g, w, up, rank, out_ref):
    rank_twice = jnp.concatenate([rank[...], rank[...]], axis=1)
    tokens = x.shape[0]
    sub = min(512, tokens)
    for i in range(tokens // sub):
        part = slice(i * sub, (i + 1) * sub)
        project_rows(x[part, :], g[part, :], w[...], up[...], rank_twice, out_ref, i, tokens)


def project_send(x, g, w, up, rank):
    tokens, depth = x.shape[0] // 2, x.shape[1]
    sub = min(512, tokens)
    steps = tokens // sub
    rows = tokens + tokens // lanes * rank.shape[0]
    vmem = pl.BlockSpec(memory_space=pltpu.VMEM)
    return pl.pallas_call(
        project_send_kernel,
        in_specs=[pl.BlockSpec(memory_space=pltpu.HBM)] * 5,
        out_specs=[vmem] * 5,
        out_shape=[
            jax.ShapeDtypeStruct((rows, lanes), bf16),
            pltpu.VMEM((tokens, depth), bf16),
            pltpu.VMEM((tokens, depth), bf16),
            pltpu.VMEM(w.shape, bf16),
            pltpu.VMEM(up.shape, bf16),
        ],
        scratch_shapes=[
            pltpu.VMEM((steps, sub, depth), bf16),
            pltpu.VMEM((steps, sub, depth), bf16),
            pltpu.VMEM(rank.shape, bf16),
            pltpu.SemaphoreType.DMA((2 * steps + 5,)),
        ],
        compiler_params=params(24),
        cost_estimate=cost(4 * tokens * depth * lanes, 8 * tokens * depth),
        name="project_send",
    )(*(pltpu.with_memory_space_constraint(array, pltpu.HBM) for array in (x, g, w, up, rank)))


def project_keep(x, g, w, up, rank):
    tokens, depth = x.shape
    rows = tokens + tokens // lanes * rank.shape[0]
    vmem = pl.BlockSpec(memory_space=pltpu.VMEM)
    return pl.pallas_call(
        project_keep_kernel,
        in_specs=[vmem] * 5,
        out_specs=vmem,
        out_shape=jax.ShapeDtypeStruct((rows, lanes), f32),
        compiler_params=params(16),
        cost_estimate=cost(4 * tokens * depth * lanes, 4 * tokens * depth),
        name="project_keep",
    )(*(pltpu.with_memory_space_constraint(array, pltpu.VMEM) for array in (x, g, w, up)), rank)


def square_kernel(targets_hbm, squares_ref, targets, sems):
    parts, rows, depth = targets.shape
    started = []
    for i in range(parts):
        part = pl.ds(i * rows, rows)
        started.append(pltpu.make_async_copy(targets_hbm.at[part, :], targets.at[i], sems.at[i]))
        started[-1].start()
    lane = lax.broadcasted_iota(jnp.int32, (lanes, lanes), 1)
    squares = jnp.zeros((lanes, lanes), f32)
    for i in range(parts):
        started[i].wait()
        for first in range(0, rows, lanes):
            totals = jnp.zeros((lanes, lanes), f32)
            for k in range(depth // lanes):
                wide = targets[i, first : first + lanes, k * lanes : (k + 1) * lanes].astype(f32)
                totals += wide * wide
            total = jnp.sum(totals, axis=1, keepdims=True)
            squares = jnp.where(lane == (i * rows + first) // lanes, total, squares)
    squares_ref[...] = squares


def column_squares(targets):
    columns, depth = targets.shape
    rows = min(256, columns)
    return pl.pallas_call(
        square_kernel,
        in_specs=[pl.BlockSpec(memory_space=pltpu.HBM)],
        out_specs=pl.BlockSpec(memory_space=pltpu.VMEM),
        out_shape=jax.ShapeDtypeStruct((lanes, lanes), f32),
        scratch_shapes=[
            pltpu.VMEM((columns // rows, rows, depth), targets.dtype),
            pltpu.SemaphoreType.DMA((columns // rows,)),
        ],
        compiler_params=params(16),
        cost_estimate=cost(2 * columns * depth, 2 * columns * depth),
        name="squares",
    )(pltpu.with_memory_space_constraint(targets, pltpu.HBM))


def stage_kernel(targets_hbm, targets_ref, sem):
    copy = pltpu.make_async_copy(targets_hbm, targets_ref, sem)
    copy.start()
    copy.wait()


def stage(targets):
    return pl.pallas_call(
        stage_kernel,
        in_specs=[pl.BlockSpec(memory_space=pltpu.HBM)],
        out_specs=pl.BlockSpec(memory_space=pltpu.VMEM),
        out_shape=pltpu.VMEM(targets.shape, targets.dtype),
        scratch_shapes=[pltpu.SemaphoreType.DMA],
        compiler_params=params(12),
        cost_estimate=cost(0, 2 * targets.size),
        name="stage",
    )(pltpu.with_memory_space_constraint(targets, pltpu.HBM))


def core_sum_kernel(parts, length, keep_ref, came_ref, *outs):
    sends, lefts = outs[:chunks], outs[chunks:]
    rows = keep_ref.shape[0]
    tokens = sum(number for _, number in parts) * length
    stack = (rows - tokens) // 2
    _, x = position()
    for (first, number), send_ref, left_ref in zip(parts, sends, lefts):
        size = number * length
        part = slice(first * length, first * length + size)
        total = keep_ref[part, :] + came_ref[part, :].astype(f32)
        send_ref[:size, :] = total.astype(bf16)
        left_ref[:size, :] = total
        height = stack * size // tokens
        for side, ref in ((1 - x, send_ref), (x, left_ref)):
            start = tokens + side * stack + stack * first * length // tokens
            part = pl.ds(pl.multiple_of(start, 32), height)
            total = keep_ref[part, :] + came_ref[part, :].astype(f32)
            ref[size:, :] = total.astype(ref.dtype)


def core_sum(keep, came, parts, length):
    rows = keep.shape[0]
    tokens = sum(number for _, number in parts) * length
    heights = [(tokens + (rows - tokens) // 2) * number * length // tokens for _, number in parts]
    vmem = pl.BlockSpec(memory_space=pltpu.VMEM)
    outs = pl.pallas_call(
        functools.partial(core_sum_kernel, parts, length),
        in_specs=[vmem, vmem],
        out_specs=[vmem] * (2 * chunks),
        out_shape=[jax.ShapeDtypeStruct((height, lanes), dtype) for dtype in (bf16, f32) for height in heights],
        compiler_params=params(8),
        cost_estimate=cost(rows * lanes, 12 * rows * lanes),
        name="core_sum",
    )(keep, came)
    return list(outs[:chunks]), list(outs[chunks:])


def feature_kernel(first, core_programs, programs, lengths, left_ref, came_ref, mine_ref, other_ref, held):
    core, _ = position()
    quarter = mine_ref.shape[0]
    out_width = 2 * quarter
    final = left_ref.shape[0]
    tokens = final * lanes // (lanes + out_width)
    length = tokens // programs
    some = 8
    span = some * length
    program = lax.broadcasted_iota(jnp.int32, (some, span), 0)
    token = lax.broadcasted_iota(jnp.int32, (some, span), 1) - program * length
    for group in range(programs // some):
        rows = slice(group * span, (group + 1) * span)
        in_sum = (left_ref[rows, :] + came_ref[rows, :].astype(f32)).astype(bf16)
        start = tokens + group * (span // lanes) * out_width
        rows = slice(start, start + span // lanes * out_width)
        out_sum = left_ref[rows, :] + came_ref[rows, :].astype(f32)
        out_rows = jnp.concatenate(
            [out_sum[i * out_width : (i + 1) * out_width, :] for i in range(span // lanes)], axis=1
        )
        limit = jnp.zeros((some, span), jnp.int32)
        for s in range(some):
            limit = jnp.where(program == s, lengths[core * core_programs + first + group * some + s], limit)
        live = ((token >= 0) & (token < limit)).astype(f32)
        spread = (out_rows[:, None, :] * live[None, :, :]).reshape(out_width * some, span)
        made = jnp.dot(spread.astype(bf16), in_sum, preferred_element_type=f32)
        held[:, group * some : (group + 1) * some, :] = made.reshape(out_width, some, lanes)
    mine_ref[...] = held[pl.ds(core * quarter, quarter), :, :].astype(bf16)
    other_ref[...] = held[pl.ds((1 - core) * quarter, quarter), :, :].astype(bf16)


def make_features(first, core_programs, programs, quarter, lengths, left, came):
    vmem = pl.BlockSpec(memory_space=pltpu.VMEM)
    shape = jax.ShapeDtypeStruct((quarter, programs, lanes), bf16)
    return pl.pallas_call(
        functools.partial(feature_kernel, first, core_programs, programs),
        in_specs=[pl.BlockSpec(memory_space=pltpu.SMEM), vmem, vmem],
        out_specs=[vmem, vmem],
        out_shape=[shape, shape],
        scratch_shapes=[pltpu.VMEM((2 * quarter, programs, lanes), f32)],
        compiler_params=params(12),
        cost_estimate=cost(10**8, 8 * left.size),
        name="features",
    )(lengths, left, came)


def score_kernel(count, far, order_ref, squares_ref, targets_ref, *refs):
    pieces, sends, (keep_ref, ordered) = refs[:count], refs[count:-2], refs[-2:]
    columns, rows = targets_ref.shape[0], keep_ref.shape[0]

    def store(first, size, values):
        height = rows // len(sends)
        for i, ref in enumerate(sends):
            ref[:, first : first + size] = values[i * height : (i + 1) * height, :]
        keep_ref[:, first : first + size] = values[rows:, :]

    core, x = position()
    x = 1 - x if far else x
    position_rows = order_ref[...]
    row = lax.broadcasted_iota(jnp.int32, (2 * rows, position_rows.shape[1]), 0)
    first = jnp.where(row < rows, (x * 2 + 1 - core) * rows, (x * 2 + core) * rows - rows)
    chosen = (row + first == position_rows).astype(bf16)
    totals = jnp.zeros((2 * rows, lanes), f32)
    halves = pieces
    while any(ref.ndim > 3 for ref in halves):
        halves = [half for ref in halves for half in ([ref.at[i] for i in range(ref.shape[0])] if ref.ndim > 3 else [ref])]
    for a in range(0, halves[0].shape[0], 2):
        block = jnp.concatenate(
            [
                jnp.concatenate([half[a + d] for half in halves], axis=0)
                for d in range(2)
            ],
            axis=1,
        )
        found = jnp.dot(chosen, block, preferred_element_type=f32)
        ordered[:, a * lanes : (a + 2) * lanes] = found.astype(bf16)
        totals += found[:, :lanes] * found[:, :lanes] + found[:, lanes:] * found[:, lanes:]
    lane = lax.broadcasted_iota(jnp.int32, (2 * rows, lanes), 1)
    row_squares = jnp.sum(totals, axis=1, keepdims=True)
    spare = jnp.zeros((rows - lanes, lanes), f32)
    squares = jnp.concatenate([squares_ref[...], spare] * 2 if rows > lanes else [squares_ref[...]] * 2, axis=0)
    store(columns, lanes, jnp.where(lane == middle, row_squares, squares).astype(bf16))
    tile = min(512, columns)
    for j in range(0, columns, tile):
        scores = lax.dot_general(
            ordered[...], targets_ref[j : j + tile, :], nt, preferred_element_type=f32
        ).astype(bf16)
        store(j, tile, scores)


def partial_scores(far, order, squares, pieces, targets, rows):
    columns, depth = targets.shape
    held = 2 * (4 * rows * depth + 4 * rows * columns + 8 * rows * order.size)
    limit = 6 + held // 1024**2
    vmem = pl.BlockSpec(memory_space=pltpu.VMEM)
    sends = 1 if far else 2
    shape = jax.ShapeDtypeStruct((rows // sends, columns + lanes), bf16)
    whole = jax.ShapeDtypeStruct((rows, columns + lanes), bf16)
    return pl.pallas_call(
        functools.partial(score_kernel, len(pieces), far),
        in_specs=[vmem] * (3 + len(pieces)),
        out_specs=[vmem] * (sends + 1),
        out_shape=[shape] * sends + [whole],
        scratch_shapes=[pltpu.VMEM((2 * rows, depth), bf16)],
        compiler_params=params(limit),
        cost_estimate=cost(4 * rows * columns * depth, 2 * columns * depth),
        name="scores_far" if far else "scores_near",
    )(order, squares, pltpu.with_memory_space_constraint(targets, pltpu.VMEM), *pieces)


def join_kernel(keep_ref, came_ref, out_ref):
    out_ref[...] = (keep_ref[...].astype(f32) + came_ref[...].astype(f32)).astype(bf16)


def join(keep, came):
    vmem = pl.BlockSpec(memory_space=pltpu.VMEM)
    return pl.pallas_call(
        join_kernel,
        in_specs=[vmem, vmem],
        out_specs=vmem,
        out_shape=jax.ShapeDtypeStruct(keep.shape, bf16),
        compiler_params=params(16),
        cost_estimate=cost(keep.size, 6 * keep.size),
        name="join",
    )(keep, came)


def finish_kernel(root_count, keep_ref, low_ref, high_ref, far_ref, out_ref):
    columns = out_ref.shape[1]
    height = low_ref.shape[0]

    def total(i, first, size):
        rows, strip = slice(i * height, (i + 1) * height), slice(first, first + size)
        mine = keep_ref[rows, strip].astype(f32) + (low_ref, high_ref)[i][:, strip].astype(f32)
        return mine + far_ref[rows, strip].astype(f32)

    squares = jnp.concatenate([total(i, columns, lanes) for i in range(2)], axis=0)
    row_scale = lax.rsqrt(squares[:, middle : middle + 1] + epsilon) * root_count
    column_scale = lax.rsqrt(squares[:lanes, :].T + epsilon)
    for i in range(2):
        rows = slice(i * height, (i + 1) * height)
        for q in range(columns // lanes):
            scaled = total(i, q * lanes, lanes) * row_scale[rows, :] * column_scale[q : q + 1, :]
            out_ref[rows, q * lanes : (q + 1) * lanes] = scaled


def finish(root_count, keep, low, high, far):
    rows, columns = keep.shape[0], keep.shape[1] - lanes
    vmem = pl.BlockSpec(memory_space=pltpu.VMEM)
    return pl.pallas_call(
        functools.partial(finish_kernel, root_count),
        in_specs=[vmem] * 4,
        out_specs=vmem,
        out_shape=jax.ShapeDtypeStruct((rows, columns), f32),
        compiler_params=params(24),
        cost_estimate=cost(4 * rows * columns, 10 * rows * columns),
        name="finish",
    )(keep, low, high, far)


def shards(
    layer_input_rows,
    output_gradient_rows,
    adapter_up_weight,
    input_side_projection,
    rank_side_projection,
    lengths,
    program_output_index,
    targets,
):
    wide_count, narrow_count = lax.axis_size("wide"), lax.axis_size("narrow")
    w, n = lax.axis_index("wide"), lax.axis_index("narrow")
    core, x = n % 2, n // 2
    programs = lengths.shape[0]
    length = layer_input_rows.shape[0] // programs
    quarter = rank_side_projection.shape[1] // narrow_count
    share = programs // 2
    parts = parts_of(share)
    rank = rank_side_projection.T
    send, *staged = project_send(
        layer_input_rows, output_gradient_rows, input_side_projection, adapter_up_weight, rank
    )
    keep = project_keep(*staged, rank)
    sends, lefts = core_sum(keep, exchange(send, "narrow", 1), parts, length)
    squares = column_squares(after(targets, sends[0]))
    lefts[0], squares = lax.optimization_barrier((lefts[0], squares))
    blocks = []
    for i in range(chunks):
        came = exchange(sends[i], "narrow", 2)
        left = after(lefts[i], *blocks) if blocks else lefts[i]
        mine, other = make_features(parts[i][0], share, parts[i][1], quarter, lengths, left, came)
        blocks.append(jnp.stack([mine, exchange(other, "narrow", 1)]))
    pieces = gather_blocks(blocks)
    targets = stage(after(targets, pieces[-2][-1]))
    pieces = [chunk for piece in pieces for chunk in piece]

    order = program_output_index.reshape(wide_count, 2, share)
    order = jnp.take(order, w ^ jnp.arange(wide_count), axis=0)
    order = jnp.where(core == 1, order[:, ::-1], order)
    order = [order[:, :, first : first + number].reshape(wide_count, -1) for first, number in parts]
    order = jnp.concatenate(order, axis=1).reshape(1, -1)
    rows = order.shape[1] // narrow_count

    far_send, far_keep = partial_scores(True, order, squares, pieces, targets, rows)
    far = join(far_keep, exchange(far_send, "narrow", 1))
    order, far = lax.optimization_barrier((order, far))
    far = exchange(far, "narrow", 2)
    *near_sends, near_keep = partial_scores(False, order, squares, pieces, targets, rows)
    near = [exchange(part, "narrow", 1) for part in near_sends]
    root_count = math.sqrt(float(targets.shape[1] * narrow_count))
    return finish(root_count, near_keep, *near, far)


def solution(mesh):
    return jax.shard_map(
        shards,
        mesh=mesh,
        in_specs=(
            P("wide", "narrow"),
            P("wide", "narrow"),
            P("narrow", None),
            P("narrow", None),
            P(),
            P("wide"),
            P(),
            P("wide", "narrow"),
        ),
        out_specs=P("narrow", "wide"),
        check_vma=False,
    )
```
